1024 devices in a mesh: replica: 32 (over y_hi, z), expert: 32 (over x, y_lo, core).
Axes of the slice: x: 4, y: 8 (y_hi: 2, y_lo: 4; y = y_hi * 4 + y_lo), z: 16, core: 2. Of those that a mesh axis runs over, the one named last changes fastest.
Arguments:
- tokens: bfloat16 [2, 65536, 2048], P(None, ('replica', 'expert')), may hold values from -6 to 6
- targets: bfloat16 [2, 65536, 2048], P(None, ('replica', 'expert')), may hold values from -6 to 6
- expert_ids: int32 [2, 65536, 1], P(None, ('replica', 'expert')), may hold values from 0 to 15; in each aligned block of 64 rows (0 to 63, 64 to 127, ..., all dimensions but the last counted through in order) at most 6 rows name the same one
- route_weight: float32 [2, 65536], P(None, ('replica', 'expert')), may hold values from 0.3 to 1
- gate_weight: bfloat16 [32, 2048, 384], P('expert'), may hold values from -6 to 6
- up_weight: bfloat16 [32, 2048, 384], P('expert'), may hold values from -6 to 6
- down_weight: bfloat16 [32, 384, 2048], P('expert'), may hold values from -6 to 6
- fragment_delta: bfloat16 [32, 32, 3, 32, 2048], P('replica', 'expert'), may hold values from -6 to 6
- global_fragment: float32 [32, 3, 32, 2048], P('expert'), may hold values from -6 to 6
- outer_momentum: float32 [32, 3, 32, 2048], P('expert'), may hold values from -2 to 2
- fragment_index: int32 [12], replicated, may hold values from 0 to 11, each once
Outputs:
- next_delta: float32 [32, 32, 3, 32, 2048], P('replica', 'expert')
- new_global: float32 [32, 3, 32, 2048], P('expert')
- new_momentum: float32 [32, 3, 32, 2048], P('expert')
The draws below stay inside these ranges and needn't reach their ends.
Inputs may be any that keep to these rules, and one draw needn't show every extreme that they name: `expert_ids`: within the rows of one device in one inner step, no expert is named more than 6 times; in some such blocks one expert is named exactly 6 times. `fragment_index`: each fragment appears exactly once.
All inputs are finite; a program needn't handle non-finite values.
Results may differ from the reference program's by a relative error of at most 0.015.
Values may be sent and summed in bfloat16 or wider, within the bound.
No kernel may reach another device: no remote copies, remote signals or barrier semaphores. Data moves between devices by JAX's collectives and lax.ppermute only.
A program may use at most 64 MiB of HBM per device.

```python
import math
import jax
import jax.numpy as jnp
import numpy as np
from jax import lax

D = 2048
F = 768
FS = 384
FRAG = 32
NFRAG = 12
TOPK = 1
TOK_DEV = 64
EXPERTS = 16
CAP = 6
TOKENS = 65536
REPLICAS = 32
N_REPLICA = 32
N_EXPERT = 32


def steps_of(own_key, shape, shards, low, largest):
    factor_of = 1.0
    for position, shards_of in shards:
        heights = jax.random.uniform(jax.random.fold_in(jax.random.fold_in(own_key, 6), position), (shards_of,), jnp.float32, low / len(shards), largest / len(shards))
        factor_of = factor_of * jnp.repeat(jnp.exp(heights), shape[position] // shards_of).reshape((-1,) + (1,) * (len(shape) - 1 - position))
    return factor_of


def deal_out(rng, own, number, rows, count, top, bound, lean):
    order = jax.random.permutation(rng, count)
    heavy_load, common = load_shares(count, rows * top, bound, lean, True), load_shares(count, rows * top, bound, lean, False)
    places = jnp.arange(count)

    def named(lengths, turn):
        used = int((lengths > 0).sum())
        fixed = max(1, used // 4)
        moved = fixed + (places - fixed + turn * (used - fixed)) % max(1, count - fixed)
        return jnp.zeros((count,), jnp.int32).at[order[jnp.where(places < fixed, places, moved)]].set(jnp.asarray(lengths, jnp.int32))

    lengths = jnp.where(number % 4 == 0, named(heavy_load, number // 4), named(common, number - number // 4 - 1))
    mixed = jax.random.permutation(jax.random.fold_in(own, 3), count)
    source_of, taker = mixed[0:count // 2 * 2:2], mixed[1:count // 2 * 2:2]
    room = jnp.minimum(lengths[source_of] - 1, bound - lengths[taker]) // 2
    room = jnp.where((source_of == order[0]) | (taker == order[0]) | (lengths[taker] == 0), 0, jnp.maximum(room, 0))
    moved = jax.random.randint(jax.random.fold_in(own, 4), (count // 2,), 0, 1 << 20) % (room + 1)
    lengths = lengths.at[source_of].add(-moved).at[taker].add(moved)
    members = jnp.searchsorted(jnp.cumsum(lengths), jnp.arange(rows * top), side="right").astype(jnp.int32)
    listing = members.reshape(top, rows).T
    listing = listing[jax.random.permutation(jax.random.fold_in(own, 1), rows)]
    turn = jax.random.randint(jax.random.fold_in(own, 2), (rows, 1), 0, top)
    return jnp.take_along_axis(listing, (jnp.arange(top)[None, :] + turn) % top, axis=1)


def load_shares(number_of, total, bound, slope, full):
    loads = [(1 << 20) // math.isqrt(rank ** slope) + 1 for rank in range(1, number_of + 1)]
    largest = bound if full else min(bound, max(-(-total // number_of), total * loads[0] // sum(loads)))
    least = 1 if total - largest >= number_of - 1 else 0
    holding, rest = [largest] + [least] * (number_of - 1), total - largest - least * (number_of - 1)
    while rest > 0:
        candidates = [i for i in range(1, number_of) if holding[i] < largest] or [i for i in range(1, number_of) if holding[i] < bound]
        whole, remaining = sum([loads[i] for i in candidates]), rest
        for i in candidates:
            addition = min(bound - holding[i], max(1, remaining * loads[i] // whole), rest)
            holding[i] = holding[i] + addition
            rest = rest - addition
    return np.array(holding)


def gaussian(key, dims, spread, reach, pieces=(), held_as=jnp.bfloat16):
    values = spread * jax.random.normal(key, dims, jnp.float32)
    if pieces:
        values = values * steps_of(key, dims, pieces, -0.22, 0.18)
    return jnp.clip(values, -reach, reach).astype(held_as)


def setup_inputs(seed: int = 0) -> dict:
    seeds = jax.random.split(jax.random.key(seed), 12)
    tokens = gaussian(seeds[0], (2, TOKENS, D), 1.0, 6.0, ((1, 1024),))
    targets = gaussian(seeds[1], (2, TOKENS, D), 1.0, 6.0, ((1, 1024),))
    expert_ids_keys = jax.random.split(jax.random.fold_in(seeds[2], 1), 2 * TOKENS // TOK_DEV)
    expert_ids_turns = jax.random.permutation(jax.random.fold_in(seeds[2], 3), 2 * TOKENS // TOK_DEV)
    expert_ids = jax.vmap(lambda own, number: deal_out(jax.random.fold_in(seeds[2], 2), own, number, TOK_DEV, EXPERTS, TOPK, CAP, 1))(expert_ids_keys, expert_ids_turns).reshape((2, TOKENS, TOPK))
    route_weight = jnp.clip(0.3 + 0.7 * jax.random.uniform(seeds[3], (2, TOKENS), jnp.float32) ** steps_of(seeds[3], (2, TOKENS), ((1, 1024),), -0.2, 0.2), 0.3, 1.0)
    gate_weight = gaussian(seeds[4], (2 * EXPERTS, D, FS), 1.0, 6.0, ((0, 32),))
    up_weight = gaussian(seeds[5], (2 * EXPERTS, D, FS), 1.0, 6.0, ((0, 32),))
    down_weight = gaussian(seeds[6], (2 * EXPERTS, FS, D), 1.0, 6.0, ((0, 32),))
    fragment_delta = gaussian(seeds[7], (REPLICAS, 2 * EXPERTS, 3, FRAG, D), 1.0, 6.0, ((0, 32), (1, 32)))
    global_fragment = gaussian(seeds[8], (2 * EXPERTS, 3, FRAG, D), 1.0, 6.0, ((0, 32),), jnp.float32)
    outer_momentum = gaussian(seeds[9], (2 * EXPERTS, 3, FRAG, D), 0.3, 2.0, ((0, 32),), jnp.float32)
    fragment_index = jax.random.permutation(seeds[10], NFRAG).astype(jnp.int32)
    return {"tokens": tokens, "targets": targets, "expert_ids": expert_ids, "route_weight": route_weight, "gate_weight": gate_weight, "up_weight": up_weight, "down_weight": down_weight, "fragment_delta": fragment_delta, "global_fragment": global_fragment, "outer_momentum": outer_momentum, "fragment_index": fragment_index}


INNER_RATE = 0.8
OUTER_RATE = 0.7
MOMENTUM = 0.9

def silu_parts(pre_act):
    sigmoid_value = jax.nn.sigmoid(pre_act)
    return (pre_act * sigmoid_value, sigmoid_value * (1.0 + pre_act * (1.0 - sigmoid_value)))

def slot_table(expert_row):
    onehot = (expert_row[:, None] == jnp.arange(EXPERTS, dtype=jnp.int32)[None, :]).astype(jnp.int32)
    before = jnp.cumsum(onehot, axis=0) - onehot
    return expert_row * CAP + lax.optimization_barrier(jnp.sum(before * onehot, axis=1))

def dispatch(values, flat_slot):
    placing = (flat_slot[:, :, None] == jnp.arange(EXPERTS * CAP, dtype=jnp.int32)[None, None, :]).astype(jnp.float32)
    table = jnp.einsum('bts,btd->sbd', placing, values.astype(jnp.float32))
    table = table.reshape(EXPERTS, CAP, N_EXPERT, D).transpose(0, 2, 1, 3).reshape(EXPERTS, N_EXPERT * CAP, D)
    return jnp.repeat(table.astype(jnp.bfloat16), 2, axis=0)

def combine(partial_rows, flat_slot):
    summed = partial_rows.reshape(EXPERTS, 2, N_EXPERT, CAP, D).sum(axis=1)
    rounded = lax.optimization_barrier(summed.astype(jnp.bfloat16)).astype(jnp.float32)
    rounded = rounded.transpose(1, 0, 2, 3).reshape(N_EXPERT, EXPERTS * CAP, D)
    return jax.vmap(lambda table_rows, index_rows: table_rows[index_rows])(rounded, flat_slot)

def expert_step(tokens_r, targets_r, ids_r, weight_r, inner_step, gate_w, up_w, down_w):
    scale_model = 1.0 / math.sqrt(D)
    scale_hidden = 1.0 / math.sqrt(F)
    flat_slot = jax.vmap(slot_table)(ids_r[inner_step])
    expert_rows = dispatch(tokens_r[inner_step], flat_slot)
    row_values = expert_rows.astype(jnp.float32)
    pre_gate = jnp.einsum('vrd,vdf->vrf', row_values, gate_w.astype(jnp.float32)) * scale_model
    pre_up = jnp.einsum('vrd,vdf->vrf', row_values, up_w.astype(jnp.float32)) * scale_model
    activated, silu_slope = silu_parts(pre_gate)
    hidden = (activated * pre_up).astype(jnp.bfloat16)
    partial_rows = jnp.einsum('vrf,vfd->vrd', hidden.astype(jnp.float32), down_w.astype(jnp.float32)) * scale_hidden
    combined = combine(partial_rows, flat_slot)
    route_column = weight_r[inner_step][:, :, None]
    output = route_column * combined
    cotangent = (route_column * (output - targets_r[inner_step].astype(jnp.float32))).astype(jnp.bfloat16)
    cotangent_rows = dispatch(cotangent, flat_slot)
    return (expert_rows, pre_gate, pre_up, activated, silu_slope, hidden, cotangent_rows)

def take_columns(weights, start_unit):
    return jnp.swapaxes(lax.dynamic_slice_in_dim(weights, start_unit, FRAG, 2), 1, 2)

def take_rows(weights, start_unit):
    return lax.dynamic_slice_in_dim(weights, start_unit, FRAG, 1)

def replica_window(tokens_r, targets_r, ids_r, weight_r, gate_w, up_w, down_w, start_unit, global_fragment):
    scale_model = 1.0 / math.sqrt(D)
    scale_hidden = 1.0 / math.sqrt(F)
    expert_rows, pre_gate, pre_up, activated, silu_slope, hidden, cotangent_rows = expert_step(tokens_r, targets_r, ids_r, weight_r, 0, gate_w, up_w, down_w)
    row_values = expert_rows.astype(jnp.float32)
    cot_values = cotangent_rows.astype(jnp.float32)
    hidden_cot = jnp.einsum('vrd,vfd->vrf', cot_values, down_w.astype(jnp.float32)) * scale_hidden
    grad_down = jnp.einsum('vrf,vrd->vfd', hidden.astype(jnp.float32), cot_values) * scale_hidden
    gate_cot = (hidden_cot * pre_up * silu_slope).astype(jnp.bfloat16)
    up_cot = (hidden_cot * activated).astype(jnp.bfloat16)
    grad_gate = jnp.einsum('vrd,vrf->vdf', row_values, gate_cot.astype(jnp.float32)) * scale_model
    grad_up = jnp.einsum('vrd,vrf->vdf', row_values, up_cot.astype(jnp.float32)) * scale_model
    first_grads = jnp.stack([take_columns(grad_gate, start_unit), take_columns(grad_up, start_unit), take_rows(grad_down, start_unit)], axis=1)
    gate_next = gate_w.astype(jnp.float32) - INNER_RATE * grad_gate
    up_next = up_w.astype(jnp.float32) - INNER_RATE * grad_up
    down_next = down_w.astype(jnp.float32) - INNER_RATE * grad_down
    expert_rows, pre_gate, pre_up, activated, silu_slope, hidden, cotangent_rows = expert_step(tokens_r, targets_r, ids_r, weight_r, 1, gate_next, up_next, down_next)
    row_values = expert_rows.astype(jnp.float32)
    cot_values = cotangent_rows.astype(jnp.float32)
    down_part = take_rows(down_next, start_unit).astype(jnp.float32)
    hidden_part = lax.dynamic_slice_in_dim(hidden, start_unit, FRAG, 2).astype(jnp.float32)
    up_part = lax.dynamic_slice_in_dim(pre_up, start_unit, FRAG, 2)
    slope_part = lax.dynamic_slice_in_dim(silu_slope, start_unit, FRAG, 2)
    act_part = lax.dynamic_slice_in_dim(activated, start_unit, FRAG, 2)
    hidden_cot = jnp.einsum('vrd,vfd->vrf', cot_values, down_part) * scale_hidden
    down_fragment = jnp.einsum('vrf,vrd->vfd', hidden_part, cot_values) * scale_hidden
    gate_cot = (hidden_cot * up_part * slope_part).astype(jnp.bfloat16)
    up_cot = (hidden_cot * act_part).astype(jnp.bfloat16)
    gate_fragment = jnp.einsum('vrf,vrd->vfd', gate_cot.astype(jnp.float32), row_values) * scale_model
    up_fragment = jnp.einsum('vrf,vrd->vfd', up_cot.astype(jnp.float32), row_values) * scale_model
    second_grads = jnp.stack([gate_fragment, up_fragment, down_fragment], axis=1)
    start_values = jnp.stack([take_columns(gate_w, start_unit), take_columns(up_w, start_unit), take_rows(down_w, start_unit)], axis=1).astype(jnp.float32)
    local_fragment = start_values - INNER_RATE * (first_grads + second_grads)
    return global_fragment - local_fragment

def reference(tokens, targets, expert_ids, route_weight, gate_weight, up_weight, down_weight, fragment_delta, global_fragment, outer_momentum, fragment_index):
    start_unit = fragment_index[0].astype(jnp.int32) * FRAG

    def split_replicas(values):
        shaped = values.reshape((2, N_REPLICA, N_EXPERT, TOK_DEV) + values.shape[2:])
        return jnp.swapaxes(shaped, 0, 1)
    per_replica = (split_replicas(tokens), split_replicas(targets), split_replicas(expert_ids[:, :, 0]), split_replicas(route_weight))

    def run_replica(items):
        return replica_window(items[0], items[1], items[2], items[3], gate_weight, up_weight, down_weight, start_unit, global_fragment)
    next_delta = lax.map(run_replica, per_replica)
    mean_delta = lax.optimization_barrier(jnp.sum(fragment_delta.astype(jnp.float32), axis=0)) / N_REPLICA
    new_momentum = MOMENTUM * outer_momentum + mean_delta
    new_global = global_fragment - OUTER_RATE * (mean_delta + MOMENTUM * new_momentum)
    return (next_delta, new_global, new_momentum)
```

```python
import functools
import math

import jax
import jax.numpy as jnp
from jax import lax
from jax.experimental import pallas as pl
from jax.experimental.pallas import tpu as pltpu
from jax.sharding import PartitionSpec as P

D = 2048
F = 768
FS = 384
FRAG = 32
EXT = 128

INNER_RATE = 0.8
OUTER_RATE = 0.7
MOMENTUM = 0.9
SCALE_MODEL = 1.0 / math.sqrt(D)
SCALE_HIDDEN = 1.0 / math.sqrt(F)
SHRINK_MODEL = INNER_RATE * SCALE_MODEL * SCALE_MODEL
SHRINK_HIDDEN = INNER_RATE * SCALE_HIDDEN * SCALE_HIDDEN

F32 = jnp.float32
BF16 = jnp.bfloat16


def iota(shape, dim):
    return lax.broadcasted_iota(jnp.int32, shape, dim)


def mm(a, b, adim=1, bdim=0, precision=None):
    return lax.dot_general(
        a, b, (((adim,), (bdim,)), ((), ())), precision=precision, preferred_element_type=F32
    )


def split_two(x):
    high = x.astype(BF16)
    return high, (x - high.astype(F32)).astype(BF16)


def silu_parts(pre):
    sig = jax.nn.sigmoid(pre)
    return pre * sig, sig * (1.0 + pre * (1.0 - sig))


def call(kernel, outs, limit=56, flops=1_000_000_000, bytes_accessed=8_000_000):
    return pl.pallas_call(
        kernel,
        out_shape=outs,
        compiler_params=pltpu.CompilerParams(vmem_limit_bytes=limit * 1024 * 1024),
        cost_estimate=pl.CostEstimate(
            flops=flops, bytes_accessed=bytes_accessed, transcendentals=0
        ),
    )


def sds(shape, dtype):
    return jax.ShapeDtypeStruct(shape, dtype)


def pack_kernel(cap, tokens, targets, ids, weight, table):
    rows = table.shape[0]
    count = 2 * tokens.shape[1]
    half = tokens.shape[1]
    ids_col = ids[...].reshape(count, 1)
    first, second = iota((count, count), 0), iota((count, count), 1)
    ids_row = jnp.sum(jnp.where(first == second, ids_col, 0), axis=0, keepdims=True)
    together = (first < half) == (second < half)
    earlier = (ids_col == ids_row) & (first < second) & together
    slot = jnp.sum(jnp.where(earlier, 1, 0), axis=0, keepdims=True)
    step_row = jnp.where(iota((1, count), 1) < half, 0, cap)
    place = ids_row * (4 * cap) + slot + step_row
    row = iota((rows, count), 0)
    put_token = (row == place).astype(BF16)
    put_target = (row == place + 2 * cap).astype(BF16)
    w_row = jnp.concatenate([weight[0:1, :], weight[1:2, :]], axis=1)
    w_col = jnp.sum(jnp.where(first == second, w_row, 0.0), axis=1, keepdims=True)
    high, rest = split_two(w_col)
    rest = w_col - high.astype(F32)
    middle = rest.astype(BF16)
    low = (rest - middle.astype(F32)).astype(BF16)
    lane = iota((count, EXT), 1)
    w_terms = jnp.where(
        lane == 0,
        high.astype(F32),
        jnp.where(lane == 1, middle.astype(F32), jnp.where(lane == 2, low.astype(F32), 0.0)),
    ).astype(BF16)
    step = 512
    for c in range(0, D, step):
        tok = tokens[:, :, c : c + step].reshape(count, step)
        tgt = targets[:, :, c : c + step].reshape(count, step)
        table[:, c : c + step] = (mm(put_token, tok) + mm(put_target, tgt)).astype(BF16)
    table[:, D : D + EXT] = mm(put_target, w_terms).astype(BF16)


def picker(cap, sources, kind):
    rows = sources * cap
    j = iota((rows, 4 * rows), 0)
    source = (j.astype(F32) * (1.0 / cap) + 0.5 / cap).astype(jnp.int32)
    wanted = j + source * (3 * cap) + kind * cap
    return (iota((rows, 4 * rows), 1) == wanted).astype(BF16)


def first_kernel(cap, own, other, gate, up, down, x_out, partial, act, slope_up, hidden_out):
    sources = own.shape[0] // (4 * cap)
    pick = picker(cap, sources, 0)
    half = sources * cap
    x_out[0:half, :] = mm(pick, own[:, 0:D]).astype(BF16)
    x_out[half:, :] = mm(pick, other[:, 0:D]).astype(BF16)
    x = x_out[...]
    pre_gate = mm(x, gate[...]) * SCALE_MODEL
    pre_up = mm(x, up[...]) * SCALE_MODEL
    activated, slope = silu_parts(pre_gate)
    act[...] = activated
    slope_up[...] = pre_up * slope
    hidden = (activated * pre_up).astype(BF16)
    hidden_out[...] = hidden
    partial[...] = mm(hidden, down[...]) * SCALE_HIDDEN


def unpack_kernel(
    cap, own, other, gate, up, x1, x2_out, t1_out, t2_out, w_out, gate_out, up_out, cross
):
    sources = own.shape[0] // (4 * cap)
    half = sources * cap
    pick = picker(cap, sources, 1)
    x2_out[0:half, :] = mm(pick, own[:, 0:D]).astype(BF16)
    x2_out[half:, :] = mm(pick, other[:, 0:D]).astype(BF16)
    for k, t_out in ((2, t1_out), (3, t2_out)):
        pick = picker(cap, sources, k)
        for part, ref in ((0, own), (half, other)):
            t_out[part : part + half, :] = mm(pick, ref[:, 0:D]).astype(BF16)
            terms = mm(pick, ref[:, D : D + EXT])
            w_out[k - 2, part : part + half, :] = jnp.broadcast_to(
                jnp.sum(terms, axis=1, keepdims=True), (half, EXT)
            )
    x2 = x2_out[...]
    gate_out[...] = mm(x2, gate[...]) * SCALE_MODEL
    up_out[...] = mm(x2, up[...]) * SCALE_MODEL
    cross[...] = mm(x2, x1[...], 1, 1)


def cotangent(partial, received, target, weight):
    half = partial.shape[0] // 2
    swapped = jnp.concatenate([received[half:, :], received[:half, :]], axis=0)
    combined = (partial + swapped).astype(BF16).astype(F32)
    return (weight * (weight * combined - target.astype(F32))).astype(BF16)


def second_kernel(
    partial, received, t1, w, down, act, slope_up, hidden1, gate2, up2, cross,
    cot_out, gate_first_out, up_first_out, partial2, hidden2_out, act2_out, slope_up2_out,
):
    cot = cotangent(partial[...], received[...], t1[...], w[0, :, 0:1])
    cot_out[...] = cot
    hidden_cot = mm(cot, down[...], 1, 1) * SCALE_HIDDEN
    gate_first = (hidden_cot * slope_up[...]).astype(BF16)
    up_first = (hidden_cot * act[...]).astype(BF16)
    gate_first_out[...] = gate_first
    up_first_out[...] = up_first
    high, low = split_two(cross[...])
    pre_gate = gate2[...] - SHRINK_MODEL * (mm(high, gate_first) + mm(low, gate_first))
    pre_up = up2[...] - SHRINK_MODEL * (mm(high, up_first) + mm(low, up_first))
    activated, slope = silu_parts(pre_gate)
    hidden = (activated * pre_up).astype(BF16)
    hidden2_out[...] = hidden
    act2_out[...] = activated
    slope_up2_out[...] = pre_up * slope
    high, low = split_two(mm(hidden, hidden1[...], 1, 1))
    partial2[...] = mm(hidden, down[...]) * SCALE_HIDDEN - SHRINK_HIDDEN * (
        mm(high, cot) + mm(low, cot)
    )


def fragment_kernel(
    index, gate, up, down, x1, cot, gate_first, up_first, hidden1, hidden2, act2, slope_up2,
    global_fragment, base, down_part, frag2, hidden_frag2,
):
    start = index[0] * FRAG
    pick = iota((FS, FRAG), 0) == iota((FS, FRAG), 1) + start
    pick_t = (iota((FRAG, FS), 1) == iota((FRAG, FS), 0) + start).astype(BF16)
    pick_f = pick.astype(F32)
    pick = pick.astype(BF16)
    gate_f = mm(gate_first[...], pick).astype(BF16)
    up_f = mm(up_first[...], pick).astype(BF16)
    hidden_f = mm(hidden1[...], pick).astype(BF16)
    base[0] = global_fragment[0] - (
        mm(pick_t, gate[...], 1, 1) - INNER_RATE * (mm(gate_f, x1[...], 0, 0) * SCALE_MODEL)
    )
    base[1] = global_fragment[1] - (
        mm(pick_t, up[...], 1, 1) - INNER_RATE * (mm(up_f, x1[...], 0, 0) * SCALE_MODEL)
    )
    down_rows = mm(pick_t, down[...])
    new_rows = down_rows - INNER_RATE * (mm(hidden_f, cot[...], 0, 0) * SCALE_HIDDEN)
    down_part[...] = new_rows
    base[2] = global_fragment[2] - new_rows
    frag2[0] = mm(slope_up2[...], pick_f, precision=lax.Precision.HIGHEST)
    frag2[1] = mm(act2[...], pick_f, precision=lax.Precision.HIGHEST)
    hidden_frag2[...] = mm(hidden2[...], pick).astype(BF16)


def last_kernel(partial, received, t2, w, x2, down_part, frag2, hidden_frag2, base, out):
    cot = cotangent(partial[...], received[...], t2[...], w[1, :, 0:1])
    high, low = split_two(down_part[...])
    hidden_cot = (mm(cot, high, 1, 1) + mm(cot, low, 1, 1)) * SCALE_HIDDEN
    gate_cot = (hidden_cot * frag2[0]).astype(BF16)
    up_cot = (hidden_cot * frag2[1]).astype(BF16)
    out[0, 0, 0] = base[0] + INNER_RATE * (mm(gate_cot, x2[...], 0, 0) * SCALE_MODEL)
    out[0, 0, 1] = base[1] + INNER_RATE * (mm(up_cot, x2[...], 0, 0) * SCALE_MODEL)
    out[0, 0, 2] = base[2] + INNER_RATE * (mm(hidden_frag2[...], cot, 0, 0) * SCALE_HIDDEN)


def replica_sum(delta):
    return lax.psum(delta, "replica").astype(F32)


def shards(
    tokens,
    targets,
    expert_ids,
    route_weight,
    gate_weight,
    up_weight,
    down_weight,
    fragment_delta,
    global_fragment,
    outer_momentum,
    fragment_index,
):
    size = lax.axis_size("expert")
    experts = size // 2
    replicas = lax.axis_size("replica")
    token_rows = tokens.shape[1]
    cap = 2 * min(token_rows // 2, max(1, token_rows * 3 // (experts * 4)))
    rows = 4 * cap * experts
    slots = 2 * cap * experts
    same_core = [[2 * e + c for e in range(experts)] for c in range(2)]
    pairs = [(i, i ^ 1) for i in range(size)]

    delta_total = replica_sum(fragment_delta[0, 0])

    table = call(functools.partial(pack_kernel, cap), sds((rows, D + EXT), BF16))(
        tokens, targets, expert_ids, route_weight
    )
    own = lax.all_to_all(
        table.reshape(experts, 4 * cap, D + EXT),
        "expert",
        split_axis=0,
        concat_axis=0,
        tiled=True,
        axis_index_groups=same_core,
    ).reshape(rows, D + EXT)
    other = lax.ppermute(own, "expert", pairs)
    gate, up, down = gate_weight[0], up_weight[0], down_weight[0]

    x1, partial, act, slope_up, hidden1 = call(
        functools.partial(first_kernel, cap),
        (
            sds((slots, D), BF16),
            sds((slots, D), F32),
            sds((slots, FS), F32),
            sds((slots, FS), F32),
            sds((slots, FS), BF16),
        ),
    )(own, other, gate, up, down)
    received = lax.ppermute(partial, "expert", pairs)
    x2, t1, t2, w, gate2, up2, cross = call(
        functools.partial(unpack_kernel, cap),
        (
            sds((slots, D), BF16),
            sds((slots, D), BF16),
            sds((slots, D), BF16),
            sds((2, slots, EXT), F32),
            sds((slots, FS), F32),
            sds((slots, FS), F32),
            sds((slots, slots), F32),
        ),
    )(own, other, gate, up, x1)
    cot, gate_first, up_first, partial2, hidden2, act2, slope_up2 = call(
        second_kernel,
        (
            sds((slots, D), BF16),
            sds((slots, FS), BF16),
            sds((slots, FS), BF16),
            sds((slots, D), F32),
            sds((slots, FS), BF16),
            sds((slots, FS), F32),
            sds((slots, FS), F32),
        ),
    )(partial, received, t1, w, down, act, slope_up, hidden1, gate2, up2, cross)
    received2 = lax.ppermute(partial2, "expert", pairs)
    base, down_part, frag2, hidden_frag2 = pl.pallas_call(
        fragment_kernel,
        out_shape=(
            sds((3, FRAG, D), F32),
            sds((FRAG, D), F32),
            sds((2, slots, FRAG), F32),
            sds((slots, FRAG), BF16),
        ),
        in_specs=[pl.BlockSpec(memory_space=pltpu.SMEM)]
        + [pl.BlockSpec(memory_space=pltpu.VMEM)] * 12,
        compiler_params=pltpu.CompilerParams(vmem_limit_bytes=56 * 1024 * 1024),
        cost_estimate=pl.CostEstimate(
            flops=1_000_000_000, bytes_accessed=8_000_000, transcendentals=0
        ),
    )(
        fragment_index, gate, up, down, x1, cot, gate_first, up_first, hidden1, hidden2, act2,
        slope_up2, global_fragment[0],
    )
    next_delta = call(last_kernel, sds((1, 1, 3, FRAG, D), F32))(
        partial2, received2, t2, w, x2, down_part, frag2, hidden_frag2, base
    )
    mean_delta = delta_total / replicas
    new_momentum = MOMENTUM * outer_momentum[0] + mean_delta
    new_global = global_fragment[0] - OUTER_RATE * (mean_delta + MOMENTUM * new_momentum)
    return (next_delta, new_global[None], new_momentum[None])


def solution(mesh):
    placed = (
        P(None, ("replica", "expert"), None),
        P(None, ("replica", "expert"), None),
        P(None, ("replica", "expert"), None),
        P(None, ("replica", "expert")),
        P("expert", None, None),
        P("expert", None, None),
        P("expert", None, None),
        P("replica", "expert", None, None, None),
        P("expert", None, None, None),
        P("expert", None, None, None),
        P(),
    )
    return jax.shard_map(
        shards,
        mesh=mesh,
        in_specs=placed,
        out_specs=(
            P("replica", "expert", None, None, None),
            P("expert", None, None, None),
            P("expert", None, None, None),
        ),
        check_vma=False,
    )
```

```python
import functools
import math

import jax
import jax.numpy as jnp
from jax import lax
from jax.experimental import pallas as pl
from jax.experimental.pallas import tpu as pltpu
from jax.sharding import PartitionSpec as P

D = 2048
F = 768
FS = 384
FRAG = 32
EXT = 128

INNER_RATE = 0.8
OUTER_RATE = 0.7
MOMENTUM = 0.9
SCALE_MODEL = 1.0 / math.sqrt(D)
SCALE_HIDDEN = 1.0 / math.sqrt(F)
SHRINK_MODEL = INNER_RATE * SCALE_MODEL * SCALE_MODEL
SHRINK_HIDDEN = INNER_RATE * SCALE_HIDDEN * SCALE_HIDDEN

F32 = jnp.float32
BF16 = jnp.bfloat16


def iota(shape, dim):
    return lax.broadcasted_iota(jnp.int32, shape, dim)


def mm(a, b, adim=1, bdim=0, precision=None):
    return lax.dot_general(
        a, b, (((adim,), (bdim,)), ((), ())), precision=precision, preferred_element_type=F32
    )


def split_two(x):
    high = x.astype(BF16)
    return high, (x - high.astype(F32)).astype(BF16)


def silu_parts(pre):
    sig = jax.nn.sigmoid(pre)
    return pre * sig, sig * (1.0 + pre * (1.0 - sig))


def call(kernel, outs, limit=20, flops=1_000, bytes_accessed=8_000):
    return pl.pallas_call(
        kernel,
        out_shape=outs,
        compiler_params=pltpu.CompilerParams(vmem_limit_bytes=limit * 1024 * 1024),
        cost_estimate=pl.CostEstimate(
            flops=flops, bytes_accessed=bytes_accessed, transcendentals=0
        ),
    )


def sds(shape, dtype):
    return jax.ShapeDtypeStruct(shape, dtype)


def pack_kernel(cap, tokens, targets, ids, weight, table):
    rows = table.shape[0]
    count = 2 * tokens.shape[1]
    half = tokens.shape[1]
    first, second = iota((count, count), 0), iota((count, count), 1)
    ids_row = jnp.concatenate([ids[0], ids[1]], axis=1)
    ids_col = jnp.sum(jnp.where(first == second, ids_row, 0), axis=1, keepdims=True)
    together = (first < half) == (second < half)
    earlier = (ids_col == ids_row) & (first < second) & together
    slot = jnp.sum(jnp.where(earlier, 1, 0), axis=0, keepdims=True)
    step_row = jnp.where(iota((1, count), 1) < half, 0, cap)
    place = ids_row * (4 * cap) + slot + step_row
    row = iota((rows, count), 0)
    put_token = (row == place).astype(BF16)
    put_target = (row == place + 2 * cap).astype(BF16)
    w_row = jnp.concatenate([weight[0:1, :], weight[1:2, :]], axis=1)
    w_col = jnp.sum(jnp.where(first == second, w_row, 0.0), axis=1, keepdims=True)
    high, rest = split_two(w_col)
    rest = w_col - high.astype(F32)
    middle = rest.astype(BF16)
    low = (rest - middle.astype(F32)).astype(BF16)
    lane = iota((count, EXT), 1)
    w_terms = jnp.where(
        lane == 0,
        high.astype(F32),
        jnp.where(lane == 1, middle.astype(F32), jnp.where(lane == 2, low.astype(F32), 0.0)),
    ).astype(BF16)
    step = 512
    for c in range(0, D, step):
        tok = tokens[:, :, c : c + step].reshape(count, step)
        tgt = targets[:, :, c : c + step].reshape(count, step)
        table[:, c : c + step] = (mm(put_token, tok) + mm(put_target, tgt)).astype(BF16)
    table[:, D : D + EXT] = mm(put_target, w_terms).astype(BF16)


def picker(cap, sources, kind):
    rows = sources * cap
    j = iota((rows, 4 * rows), 0)
    source = (j.astype(F32) * (1.0 / cap) + 0.5 / cap).astype(jnp.int32)
    wanted = j + source * (3 * cap) + kind * cap
    return (iota((rows, 4 * rows), 1) == wanted).astype(BF16)


def first_kernel(
    cap, own, other, gate, up, down, x_out, partial, sent, act, slope_up, hidden_out
):
    sources = own.shape[0] // (4 * cap)
    pick = picker(cap, sources, 0)
    half = sources * cap
    x_out[0:half, :] = mm(pick, own[:, 0:D]).astype(BF16)
    x_out[half:, :] = mm(pick, other[:, 0:D]).astype(BF16)
    x = x_out[...]
    pre_gate = mm(x, gate[...]) * SCALE_MODEL
    pre_up = mm(x, up[...]) * SCALE_MODEL
    activated, slope = silu_parts(pre_gate)
    act[...] = activated
    slope_up[...] = pre_up * slope
    hidden = (activated * pre_up).astype(BF16)
    hidden_out[...] = hidden
    result = mm(hidden, down[...]) * SCALE_HIDDEN
    partial[...] = result
    sent[...] = result.astype(BF16)


def unpack_kernel(
    cap, own, other, gate, up, x1, x2_out, t1_out, t2_out, w_out, gate_out, up_out, cross
):
    sources = own.shape[0] // (4 * cap)
    half = sources * cap
    pick = picker(cap, sources, 1)
    x2_out[0:half, :] = mm(pick, own[:, 0:D]).astype(BF16)
    x2_out[half:, :] = mm(pick, other[:, 0:D]).astype(BF16)
    for k, t_out in ((2, t1_out), (3, t2_out)):
        pick = picker(cap, sources, k)
        for part, ref in ((0, own), (half, other)):
            t_out[part : part + half, :] = mm(pick, ref[:, 0:D]).astype(BF16)
            terms = mm(pick, ref[:, D : D + EXT])
            w_out[k - 2, part : part + half, :] = jnp.broadcast_to(
                jnp.sum(terms, axis=1, keepdims=True), (half, EXT)
            )
    x2 = x2_out[...]
    gate_out[...] = mm(x2, gate[...]) * SCALE_MODEL
    up_out[...] = mm(x2, up[...]) * SCALE_MODEL
    cross[...] = mm(x2, x1[...], 1, 1)


def cotangent(partial, received, target, weight):
    half = partial.shape[0] // 2
    swapped = jnp.concatenate([received[half:, :], received[:half, :]], axis=0)
    combined = (partial + swapped.astype(F32)).astype(BF16).astype(F32)
    return (weight * (weight * combined - target.astype(F32))).astype(BF16)


def second_kernel(
    partial, received, t1, w, down, act, slope_up, hidden1, gate2, up2, cross,
    cot_out, gate_first_out, up_first_out, partial2, sent, hidden2_out, act2_out, slope_up2_out,
):
    cot = cotangent(partial[...], received[...], t1[...], w[0, :, 0:1])
    cot_out[...] = cot
    hidden_cot = mm(cot, down[...], 1, 1) * SCALE_HIDDEN
    gate_first = (hidden_cot * slope_up[...]).astype(BF16)
    up_first = (hidden_cot * act[...]).astype(BF16)
    gate_first_out[...] = gate_first
    up_first_out[...] = up_first
    high, low = split_two(cross[...])
    pre_gate = gate2[...] - SHRINK_MODEL * (mm(high, gate_first) + mm(low, gate_first))
    pre_up = up2[...] - SHRINK_MODEL * (mm(high, up_first) + mm(low, up_first))
    activated, slope = silu_parts(pre_gate)
    hidden = (activated * pre_up).astype(BF16)
    hidden2_out[...] = hidden
    act2_out[...] = activated
    slope_up2_out[...] = pre_up * slope
    high, low = split_two(mm(hidden, hidden1[...], 1, 1))
    result = mm(hidden, down[...]) * SCALE_HIDDEN - SHRINK_HIDDEN * (mm(high, cot) + mm(low, cot))
    partial2[...] = result
    sent[...] = result.astype(BF16)


def fragment_kernel(
    index, gate, up, down, x1, cot, gate_first, up_first, hidden1, hidden2, act2, slope_up2,
    global_fragment, base, down_part, frag2, hidden_frag2,
):
    start = index[0] * FRAG
    pick = iota((FS, FRAG), 0) == iota((FS, FRAG), 1) + start
    pick_t = (iota((FRAG, FS), 1) == iota((FRAG, FS), 0) + start).astype(BF16)
    pick_f = pick.astype(F32)
    pick = pick.astype(BF16)
    gate_f = mm(gate_first[...], pick).astype(BF16)
    up_f = mm(up_first[...], pick).astype(BF16)
    hidden_f = mm(hidden1[...], pick).astype(BF16)
    base[0] = global_fragment[0] - (
        mm(pick_t, gate[...], 1, 1) - INNER_RATE * (mm(gate_f, x1[...], 0, 0) * SCALE_MODEL)
    )
    base[1] = global_fragment[1] - (
        mm(pick_t, up[...], 1, 1) - INNER_RATE * (mm(up_f, x1[...], 0, 0) * SCALE_MODEL)
    )
    down_rows = mm(pick_t, down[...])
    new_rows = down_rows - INNER_RATE * (mm(hidden_f, cot[...], 0, 0) * SCALE_HIDDEN)
    down_part[...] = new_rows
    base[2] = global_fragment[2] - new_rows
    frag2[0] = mm(slope_up2[...], pick_f, precision=lax.Precision.HIGHEST)
    frag2[1] = mm(act2[...], pick_f, precision=lax.Precision.HIGHEST)
    hidden_frag2[...] = mm(hidden2[...], pick).astype(BF16)


def last_kernel(partial, received, t2, w, x2, down_part, frag2, hidden_frag2, base, out):
    cot = cotangent(partial[...], received[...], t2[...], w[1, :, 0:1])
    high, low = split_two(down_part[...])
    hidden_cot = (mm(cot, high, 1, 1) + mm(cot, low, 1, 1)) * SCALE_HIDDEN
    gate_cot = (hidden_cot * frag2[0]).astype(BF16)
    up_cot = (hidden_cot * frag2[1]).astype(BF16)
    out[0, 0, 0] = base[0] + INNER_RATE * (mm(gate_cot, x2[...], 0, 0) * SCALE_MODEL)
    out[0, 0, 1] = base[1] + INNER_RATE * (mm(up_cot, x2[...], 0, 0) * SCALE_MODEL)
    out[0, 0, 2] = base[2] + INNER_RATE * (mm(hidden_frag2[...], cot, 0, 0) * SCALE_HIDDEN)


def inner_of(replicas):
    return min(replicas, 8)


def outer_of(replicas):
    return min(replicas, 16)


def lane_of(place, inner, lanes):
    lane = 0
    while inner > 1:
        lanes //= 2
        lane += place % 2 * lanes
        place //= 2
        inner //= 2
    return lane


def halve(values, distance):
    replicas = lax.axis_size("replica")
    half = values.shape[1] // 2
    bit = lax.bitwise_and(lax.axis_index("replica") // distance, 1)
    sent = lax.dynamic_slice_in_dim(values, (1 - bit) * half, half, 1)
    kept = lax.dynamic_slice_in_dim(values, bit * half, half, 1)
    if half > 256:
        sent = sent.astype(BF16)
    got = lax.ppermute(sent, "replica", [(i, i ^ distance) for i in range(replicas)])
    return kept, got


def scatter_sum(values, inner, span):
    distance = 2
    while distance < inner:
        kept, got = halve(values, distance)
        values = kept + got.astype(F32)
        distance *= 2
    replicas = lax.axis_size("replica")
    distance = span
    while distance < replicas:
        got = lax.ppermute(values, "replica", [(i, i ^ distance) for i in range(replicas)])
        values = values + got
        distance *= 2
    return values.astype(BF16)


def outer_kernel(replicas, pieces, global_fragment, momentum, new_global, new_momentum):
    span, _, width = pieces.shape
    lanes = global_fragment.shape[1]
    inner = lanes // width
    for place in range(inner):
        lane = lane_of(place, inner, lanes)
        at = (slice(None), slice(lane, lane + width))
        total = pieces[place].astype(F32)
        for other in range(place + inner, span, inner):
            total += pieces[other].astype(F32)
        mean = total * (1.0 / replicas)
        moved = MOMENTUM * momentum[at] + mean
        new_momentum[at] = moved
        new_global[at] = global_fragment[at] - OUTER_RATE * (mean + MOMENTUM * moved)


def shards(
    tokens,
    targets,
    expert_ids,
    route_weight,
    gate_weight,
    up_weight,
    down_weight,
    fragment_delta,
    global_fragment,
    outer_momentum,
    fragment_index,
):
    size = lax.axis_size("expert")
    experts = size // 2
    replicas = lax.axis_size("replica")
    token_rows = tokens.shape[1]
    cap = 2 * min(token_rows // 2, max(1, token_rows * 3 // (experts * 4)))
    rows = 4 * cap * experts
    slots = 2 * cap * experts
    same_core = [[2 * e + c for e in range(experts)] for c in range(2)]
    pairs = [(i, i ^ 1) for i in range(size)]

    inner, span = inner_of(replicas), outer_of(replicas)
    kept, got = halve(fragment_delta.reshape(3 * FRAG, D), 1)

    table = call(functools.partial(pack_kernel, cap), sds((rows, D + EXT), BF16), 56)(
        tokens, targets, expert_ids.transpose(0, 2, 1), route_weight
    )
    table, got = lax.optimization_barrier((table, got))
    piece = scatter_sum(kept.astype(F32) + got.astype(F32), inner, span)
    own = lax.all_to_all(
        table.reshape(experts, 4 * cap, D + EXT),
        "expert",
        split_axis=0,
        concat_axis=0,
        tiled=True,
        axis_index_groups=same_core,
    ).reshape(rows, D + EXT)
    own, piece = lax.optimization_barrier((own, piece))
    pieces = lax.all_to_all(
        jnp.broadcast_to(piece[None], (span,) + piece.shape),
        "replica",
        split_axis=0,
        concat_axis=0,
        tiled=True,
        axis_index_groups=[
            list(range(start, start + span)) for start in range(0, replicas, span)
        ],
    )
    other = lax.ppermute(own, "expert", pairs)
    gate, up, down = gate_weight[0], up_weight[0], down_weight[0]

    x1, partial, sent, act, slope_up, hidden1 = call(
        functools.partial(first_kernel, cap),
        (
            sds((slots, D), BF16),
            sds((slots, D), F32),
            sds((slots, D), BF16),
            sds((slots, FS), F32),
            sds((slots, FS), F32),
            sds((slots, FS), BF16),
        ),
    )(own, other, gate, up, down)
    received = lax.ppermute(sent, "expert", pairs)
    x2, t1, t2, w, gate2, up2, cross = call(
        functools.partial(unpack_kernel, cap),
        (
            sds((slots, D), BF16),
            sds((slots, D), BF16),
            sds((slots, D), BF16),
            sds((2, slots, EXT), F32),
            sds((slots, FS), F32),
            sds((slots, FS), F32),
            sds((slots, slots), F32),
        ),
    )(own, other, gate, up, x1)
    cot, gate_first, up_first, partial2, sent2, hidden2, act2, slope_up2 = call(
        second_kernel,
        (
            sds((slots, D), BF16),
            sds((slots, FS), BF16),
            sds((slots, FS), BF16),
            sds((slots, D), F32),
            sds((slots, D), BF16),
            sds((slots, FS), BF16),
            sds((slots, FS), F32),
            sds((slots, FS), F32),
        ),
    )(partial, received, t1, w, down, act, slope_up, hidden1, gate2, up2, cross)
    received2 = lax.ppermute(sent2, "expert", pairs)
    base, down_part, frag2, hidden_frag2 = pl.pallas_call(
        fragment_kernel,
        out_shape=(
            sds((3, FRAG, D), F32),
            sds((FRAG, D), F32),
            sds((2, slots, FRAG), F32),
            sds((slots, FRAG), BF16),
        ),
        in_specs=[pl.BlockSpec(memory_space=pltpu.SMEM)]
        + [pl.BlockSpec(memory_space=pltpu.VMEM)] * 12,
        compiler_params=pltpu.CompilerParams(vmem_limit_bytes=20 * 1024 * 1024),
        cost_estimate=pl.CostEstimate(
            flops=1_000, bytes_accessed=8_000, transcendentals=0
        ),
    )(
        fragment_index, gate, up, down, x1, cot, gate_first, up_first, hidden1, hidden2, act2,
        slope_up2, global_fragment[0],
    )
    next_delta = call(last_kernel, sds((1, 1, 3, FRAG, D), F32))(
        partial2, received2, t2, w, x2, down_part, frag2, hidden_frag2, base
    )
    next_delta, pieces = lax.optimization_barrier((next_delta, pieces))
    new_global, new_momentum = call(
        functools.partial(outer_kernel, replicas),
        (sds((3 * FRAG, D), F32), sds((3 * FRAG, D), F32)),
    )(pieces, global_fragment.reshape(3 * FRAG, D), outer_momentum.reshape(3 * FRAG, D))
    whole = (1, 3, FRAG, D)
    return (next_delta, new_global.reshape(whole), new_momentum.reshape(whole))


def solution(mesh):
    placed = (
        P(None, ("replica", "expert"), None),
        P(None, ("replica", "expert"), None),
        P(None, ("replica", "expert"), None),
        P(None, ("replica", "expert")),
        P("expert", None, None),
        P("expert", None, None),
        P("expert", None, None),
        P("replica", "expert", None, None, None),
        P("expert", None, None, None),
        P("expert", None, None, None),
        P(),
    )
    return jax.shard_map(
        shards,
        mesh=mesh,
        in_specs=placed,
        out_specs=(
            P("replica", "expert", None, None, None),
            P("expert", None, None, None),
            P("expert", None, None, None),
        ),
        check_vma=False,
    )
```

```python
import functools
import math

import jax
import jax.numpy as jnp
from jax import lax
from jax.experimental import pallas as pl
from jax.experimental.pallas import tpu as pltpu
from jax.sharding import PartitionSpec as P

D = 2048
F = 768
FS = 384
FRAG = 32
EXT = 128

INNER_RATE = 0.8
OUTER_RATE = 0.7
MOMENTUM = 0.9
SCALE_MODEL = 1.0 / math.sqrt(D)
SCALE_HIDDEN = 1.0 / math.sqrt(F)
SHRINK_MODEL = INNER_RATE * SCALE_MODEL * SCALE_MODEL
SHRINK_HIDDEN = INNER_RATE * SCALE_HIDDEN * SCALE_HIDDEN

F32 = jnp.float32
BF16 = jnp.bfloat16


def iota(shape, dim):
    return lax.broadcasted_iota(jnp.int32, shape, dim)


def mm(a, b, adim=1, bdim=0, precision=None):
    return lax.dot_general(
        a, b, (((adim,), (bdim,)), ((), ())), precision=precision, preferred_element_type=F32
    )


def split_two(x):
    high = x.astype(BF16)
    return high, (x - high.astype(F32)).astype(BF16)


def silu_parts(pre):
    sig = jax.nn.sigmoid(pre)
    return pre * sig, sig * (1.0 + pre * (1.0 - sig))


def call(kernel, outs, limit=20, flops=1_000_000_000, bytes_accessed=10_000_000):
    return pl.pallas_call(
        kernel,
        out_shape=outs,
        compiler_params=pltpu.CompilerParams(vmem_limit_bytes=limit * 1024 * 1024),
        cost_estimate=pl.CostEstimate(
            flops=flops, bytes_accessed=bytes_accessed, transcendentals=0
        ),
    )


def sds(shape, dtype):
    return jax.ShapeDtypeStruct(shape, dtype)


def pack_kernel(cap, tokens, targets, ids, weight, table):
    rows = table.shape[0]
    count = 2 * tokens.shape[1]
    half = tokens.shape[1]
    first, second = iota((count, count), 0), iota((count, count), 1)
    ids_row = jnp.concatenate([ids[0], ids[1]], axis=1)
    ids_col = jnp.sum(jnp.where(first == second, ids_row, 0), axis=1, keepdims=True)
    together = (first < half) == (second < half)
    earlier = (ids_col == ids_row) & (first < second) & together
    slot = jnp.sum(jnp.where(earlier, 1, 0), axis=0, keepdims=True)
    step_row = jnp.where(iota((1, count), 1) < half, 0, cap)
    place = ids_row * (4 * cap) + slot + step_row
    row = iota((rows, count), 0)
    put_token = (row == place).astype(BF16)
    put_target = (row == place + 2 * cap).astype(BF16)
    w_row = jnp.concatenate([weight[0:1, :], weight[1:2, :]], axis=1)
    w_col = jnp.sum(jnp.where(first == second, w_row, 0.0), axis=1, keepdims=True)
    high, rest = split_two(w_col)
    rest = w_col - high.astype(F32)
    middle = rest.astype(BF16)
    low = (rest - middle.astype(F32)).astype(BF16)
    lane = iota((count, EXT), 1)
    w_terms = jnp.where(
        lane == 0,
        high.astype(F32),
        jnp.where(lane == 1, middle.astype(F32), jnp.where(lane == 2, low.astype(F32), 0.0)),
    ).astype(BF16)
    step = 512
    for c in range(0, D, step):
        tok = tokens[:, :, c : c + step].reshape(count, step)
        tgt = targets[:, :, c : c + step].reshape(count, step)
        table[:, c : c + step] = (mm(put_token, tok) + mm(put_target, tgt)).astype(BF16)
    table[:, D : D + EXT] = mm(put_target, w_terms).astype(BF16)


def picker(cap, sources, kind):
    rows = sources * cap
    j = iota((rows, 4 * rows), 0)
    source = (j.astype(F32) * (1.0 / cap) + 0.5 / cap).astype(jnp.int32)
    wanted = j + source * (3 * cap) + kind * cap
    return (iota((rows, 4 * rows), 1) == wanted).astype(BF16)


def first_kernel(
    cap, own, other, gate, up, down, x_out, partial, sent, act, slope_up, hidden_out
):
    sources = own.shape[0] // (4 * cap)
    pick = picker(cap, sources, 0)
    half = sources * cap
    x_out[0:half, :] = mm(pick, own[:, 0:D]).astype(BF16)
    x_out[half:, :] = mm(pick, other[:, 0:D]).astype(BF16)
    x = x_out[...]
    pre_gate = mm(x, gate[...]) * SCALE_MODEL
    pre_up = mm(x, up[...]) * SCALE_MODEL
    activated, slope = silu_parts(pre_gate)
    act[...] = activated
    slope_up[...] = pre_up * slope
    hidden = (activated * pre_up).astype(BF16)
    hidden_out[...] = hidden
    result = mm(hidden, down[...]) * SCALE_HIDDEN
    partial[...] = result
    sent[...] = result.astype(BF16)


def unpack_kernel(
    cap, own, other, gate, up, x1, x2_out, t1_out, t2_out, w_out, gate_out, up_out, cross
):
    sources = own.shape[0] // (4 * cap)
    half = sources * cap
    pick = picker(cap, sources, 1)
    x2_out[0:half, :] = mm(pick, own[:, 0:D]).astype(BF16)
    x2_out[half:, :] = mm(pick, other[:, 0:D]).astype(BF16)
    for k, t_out in ((2, t1_out), (3, t2_out)):
        pick = picker(cap, sources, k)
        for part, ref in ((0, own), (half, other)):
            t_out[part : part + half, :] = mm(pick, ref[:, 0:D]).astype(BF16)
            terms = mm(pick, ref[:, D : D + EXT])
            w_out[k - 2, part : part + half, :] = jnp.broadcast_to(
                jnp.sum(terms, axis=1, keepdims=True), (half, EXT)
            )
    x2 = x2_out[...]
    gate_out[...] = mm(x2, gate[...]) * SCALE_MODEL
    up_out[...] = mm(x2, up[...]) * SCALE_MODEL
    cross[...] = mm(x2, x1[...], 1, 1)


def cotangent(partial, received, target, weight):
    half = partial.shape[0] // 2
    swapped = jnp.concatenate([received[half:, :], received[:half, :]], axis=0)
    combined = (partial + swapped.astype(F32)).astype(BF16).astype(F32)
    return (weight * (weight * combined - target.astype(F32))).astype(BF16)


def second_kernel(
    partial, received, t1, w, down, act, slope_up, hidden1, gate2, up2, cross,
    cot_out, gate_first_out, up_first_out, partial2, sent, hidden2_out, act2_out, slope_up2_out,
):
    cot = cotangent(partial[...], received[...], t1[...], w[0, :, 0:1])
    cot_out[...] = cot
    hidden_cot = mm(cot, down[...], 1, 1) * SCALE_HIDDEN
    gate_first = (hidden_cot * slope_up[...]).astype(BF16)
    up_first = (hidden_cot * act[...]).astype(BF16)
    gate_first_out[...] = gate_first
    up_first_out[...] = up_first
    high, low = split_two(cross[...])
    pre_gate = gate2[...] - SHRINK_MODEL * (mm(high, gate_first) + mm(low, gate_first))
    pre_up = up2[...] - SHRINK_MODEL * (mm(high, up_first) + mm(low, up_first))
    activated, slope = silu_parts(pre_gate)
    hidden = (activated * pre_up).astype(BF16)
    hidden2_out[...] = hidden
    act2_out[...] = activated
    slope_up2_out[...] = pre_up * slope
    high, low = split_two(mm(hidden, hidden1[...], 1, 1))
    result = mm(hidden, down[...]) * SCALE_HIDDEN - SHRINK_HIDDEN * (mm(high, cot) + mm(low, cot))
    partial2[...] = result
    sent[...] = result.astype(BF16)


def fragment_kernel(
    index, gate, up, down, x1, cot, gate_first, up_first, hidden1, hidden2, act2, slope_up2,
    global_fragment, base, down_part, frag2, hidden_frag2,
):
    start = index[0] * FRAG
    pick = iota((FS, FRAG), 0) == iota((FS, FRAG), 1) + start
    pick_t = (iota((FRAG, FS), 1) == iota((FRAG, FS), 0) + start).astype(BF16)
    pick_f = pick.astype(F32)
    pick = pick.astype(BF16)
    gate_f = mm(gate_first[...], pick).astype(BF16)
    up_f = mm(up_first[...], pick).astype(BF16)
    hidden_f = mm(hidden1[...], pick).astype(BF16)
    base[0] = global_fragment[0] - (
        mm(pick_t, gate[...], 1, 1) - INNER_RATE * (mm(gate_f, x1[...], 0, 0) * SCALE_MODEL)
    )
    base[1] = global_fragment[1] - (
        mm(pick_t, up[...], 1, 1) - INNER_RATE * (mm(up_f, x1[...], 0, 0) * SCALE_MODEL)
    )
    down_rows = mm(pick_t, down[...])
    new_rows = down_rows - INNER_RATE * (mm(hidden_f, cot[...], 0, 0) * SCALE_HIDDEN)
    down_part[...] = new_rows
    base[2] = global_fragment[2] - new_rows
    frag2[0] = mm(slope_up2[...], pick_f, precision=lax.Precision.HIGHEST)
    frag2[1] = mm(act2[...], pick_f, precision=lax.Precision.HIGHEST)
    hidden_frag2[...] = mm(hidden2[...], pick).astype(BF16)


def last_kernel(partial, received, t2, w, x2, down_part, frag2, hidden_frag2, base, out):
    cot = cotangent(partial[...], received[...], t2[...], w[1, :, 0:1])
    high, low = split_two(down_part[...])
    hidden_cot = (mm(cot, high, 1, 1) + mm(cot, low, 1, 1)) * SCALE_HIDDEN
    gate_cot = (hidden_cot * frag2[0]).astype(BF16)
    up_cot = (hidden_cot * frag2[1]).astype(BF16)
    out[0, 0, 0] = base[0] + INNER_RATE * (mm(gate_cot, x2[...], 0, 0) * SCALE_MODEL)
    out[0, 0, 1] = base[1] + INNER_RATE * (mm(up_cot, x2[...], 0, 0) * SCALE_MODEL)
    out[0, 0, 2] = base[2] + INNER_RATE * (mm(hidden_frag2[...], cot, 0, 0) * SCALE_HIDDEN)


def inner_of(replicas):
    return min(replicas, 8)


def mask_of(distance):
    return 12 if distance == 8 else distance


def pick_of(place, distance):
    bit = (place // distance) & 1
    return bit ^ ((place // 8) & 1) if distance == 4 else bit


def swap(values, distance):
    replicas = lax.axis_size("replica")
    return lax.ppermute(values, "replica", [(i, i ^ distance) for i in range(replicas)])


def halve(values, distance):
    half = values.shape[1] // 2
    bit = pick_of(lax.axis_index("replica"), distance)
    sent = lax.dynamic_slice_in_dim(values, (1 - bit) * half, half, 1)
    kept = lax.dynamic_slice_in_dim(values, bit * half, half, 1)
    return kept, swap(sent.astype(BF16), distance)


def add_across(values, distance):
    mine = values.astype(BF16)
    return mine.astype(F32) + swap(mine, mask_of(distance)).astype(F32)


def outer_kernel(replicas, marks, me, held_pieces, got_pieces, global_fragment, momentum,
                 new_global, new_momentum):
    rows, lanes = global_fragment.shape
    width = held_pieces.shape[1]
    here = len(marks) // 2 if len(marks) > 1 else 1
    for j, mark in enumerate(marks):
        place = me[0] ^ mark
        lane, step, distance = 0, lanes // 2, 1
        while step >= width:
            lane = lane + pick_of(place, distance) * step
            step //= 2
            distance *= 2
        at = (slice(None), pl.ds(pl.multiple_of(lane, 128), width))
        source, k = (held_pieces, j) if j < here else (got_pieces, j - here)
        mean = source[k * rows : (k + 1) * rows, :].astype(F32) * (1.0 / replicas)
        moved = MOMENTUM * momentum[at] + mean
        new_momentum[at] = moved
        new_global[at] = global_fragment[at] - OUTER_RATE * (mean + MOMENTUM * moved)


def shards(
    tokens,
    targets,
    expert_ids,
    route_weight,
    gate_weight,
    up_weight,
    down_weight,
    fragment_delta,
    global_fragment,
    outer_momentum,
    fragment_index,
):
    size = lax.axis_size("expert")
    experts = size // 2
    replicas = lax.axis_size("replica")
    token_rows = tokens.shape[1]
    cap = 2 * min(token_rows // 2, max(1, token_rows * 3 // (experts * 4)))
    rows = 4 * cap * experts
    slots = 2 * cap * experts
    same_core = [[2 * e + c for e in range(experts)] for c in range(2)]
    pairs = [(i, i ^ 1) for i in range(size)]

    inner = inner_of(replicas)
    kept, got = halve(fragment_delta.reshape(3 * FRAG, D), 1)

    table = call(functools.partial(pack_kernel, cap), sds((rows, D + EXT), BF16), 56)(
        tokens, targets, expert_ids.transpose(0, 2, 1), route_weight
    )
    table, got = lax.optimization_barrier((table, got))
    sums = kept.astype(F32) + got.astype(F32)
    distance = 2
    while distance < inner:
        kept, got = halve(sums, distance)
        sums = kept + got.astype(F32)
        distance *= 2
    across = []
    while distance < replicas:
        across.insert(0, distance)
        distance *= 2
    for distance in across:
        sums = add_across(sums, distance)
    pieces = sums.astype(BF16)
    own = lax.all_to_all(
        table.reshape(experts, 4 * cap, D + EXT),
        "expert",
        split_axis=0,
        concat_axis=0,
        tiled=True,
        axis_index_groups=same_core,
    ).reshape(rows, D + EXT)
    own, pieces = lax.optimization_barrier((own, pieces))
    other = lax.ppermute(own, "expert", pairs)
    gather = [inner >> k for k in range(1, inner.bit_length())]
    marks = [0]
    for distance in gather:
        marks += [mark ^ distance for mark in marks]
    held = []
    for distance in gather[:-2]:
        held.append(swap(pieces, distance))
    gate, up, down = gate_weight[0], up_weight[0], down_weight[0]

    x1, partial, sent, act, slope_up, hidden1 = call(
        functools.partial(first_kernel, cap),
        (
            sds((slots, D), BF16),
            sds((slots, D), F32),
            sds((slots, D), BF16),
            sds((slots, FS), F32),
            sds((slots, FS), F32),
            sds((slots, FS), BF16),
        ),
    )(own, other, gate, up, down)
    sent, *held = lax.optimization_barrier((sent, *held))
    for got in held:
        pieces = jnp.concatenate([pieces, got], axis=0)
    received = lax.ppermute(sent, "expert", pairs)
    held = [swap(pieces, distance) for distance in gather[-2:-1]]
    x2, t1, t2, w, gate2, up2, cross = call(
        functools.partial(unpack_kernel, cap),
        (
            sds((slots, D), BF16),
            sds((slots, D), BF16),
            sds((slots, D), BF16),
            sds((2, slots, EXT), F32),
            sds((slots, FS), F32),
            sds((slots, FS), F32),
            sds((slots, slots), F32),
        ),
    )(own, other, gate, up, x1)
    cot, gate_first, up_first, partial2, sent2, hidden2, act2, slope_up2 = call(
        second_kernel,
        (
            sds((slots, D), BF16),
            sds((slots, FS), BF16),
            sds((slots, FS), BF16),
            sds((slots, D), F32),
            sds((slots, D), BF16),
            sds((slots, FS), BF16),
            sds((slots, FS), F32),
            sds((slots, FS), F32),
        ),
    )(partial, received, t1, w, down, act, slope_up, hidden1, gate2, up2, cross)
    sent2, *held = lax.optimization_barrier((sent2, *held))
    for got in held:
        pieces = jnp.concatenate([pieces, got], axis=0)
    received2 = lax.ppermute(sent2, "expert", pairs)
    got = pieces
    for distance in gather[-1:]:
        got = swap(pieces, distance)
    base, down_part, frag2, hidden_frag2 = pl.pallas_call(
        fragment_kernel,
        out_shape=(
            sds((3, FRAG, D), F32),
            sds((FRAG, D), F32),
            sds((2, slots, FRAG), F32),
            sds((slots, FRAG), BF16),
        ),
        in_specs=[pl.BlockSpec(memory_space=pltpu.SMEM)]
        + [pl.BlockSpec(memory_space=pltpu.VMEM)] * 12,
        compiler_params=pltpu.CompilerParams(vmem_limit_bytes=20 * 1024 * 1024),
        cost_estimate=pl.CostEstimate(
            flops=1_000_000_000, bytes_accessed=10_000_000, transcendentals=0
        ),
    )(
        fragment_index, gate, up, down, x1, cot, gate_first, up_first, hidden1, hidden2, act2,
        slope_up2, global_fragment[0],
    )
    next_delta = call(last_kernel, sds((1, 1, 3, FRAG, D), F32))(
        partial2, received2, t2, w, x2, down_part, frag2, hidden_frag2, base
    )
    next_delta, got = lax.optimization_barrier((next_delta, got))
    new_global, new_momentum = pl.pallas_call(
        functools.partial(outer_kernel, replicas, tuple(marks)),
        out_shape=(sds((3 * FRAG, D), F32), sds((3 * FRAG, D), F32)),
        in_specs=[pl.BlockSpec(memory_space=pltpu.SMEM)]
        + [pl.BlockSpec(memory_space=pltpu.VMEM)] * 4,
        compiler_params=pltpu.CompilerParams(vmem_limit_bytes=20 * 1024 * 1024),
        cost_estimate=pl.CostEstimate(flops=1_000_000_000, bytes_accessed=10_000_000, transcendentals=0),
    )(
        lax.axis_index("replica").astype(jnp.int32).reshape(1),
        pieces,
        got,
        global_fragment.reshape(3 * FRAG, D),
        outer_momentum.reshape(3 * FRAG, D),
    )
    whole = (1, 3, FRAG, D)
    return (next_delta, new_global.reshape(whole), new_momentum.reshape(whole))


def solution(mesh):
    placed = (
        P(None, ("replica", "expert"), None),
        P(None, ("replica", "expert"), None),
        P(None, ("replica", "expert"), None),
        P(None, ("replica", "expert")),
        P("expert", None, None),
        P("expert", None, None),
        P("expert", None, None),
        P("replica", "expert", None, None, None),
        P("expert", None, None, None),
        P("expert", None, None, None),
        P(),
    )
    return jax.shard_map(
        shards,
        mesh=mesh,
        in_specs=placed,
        out_specs=(
            P("replica", "expert", None, None, None),
            P("expert", None, None, None),
            P("expert", None, None, None),
        ),
        check_vma=False,
    )
```

```python
import functools
import math

import jax
import jax.numpy as jnp
from jax import lax
from jax.experimental import pallas as pl
from jax.experimental.pallas import tpu as pltpu
from jax.sharding import PartitionSpec as P

D = 2048
F = 768
FS = 384
FRAG = 32
EXT = 128

INNER_RATE = 0.8
OUTER_RATE = 0.7
MOMENTUM = 0.9
SCALE_MODEL = 1.0 / math.sqrt(D)
SCALE_HIDDEN = 1.0 / math.sqrt(F)
SHRINK_MODEL = INNER_RATE * SCALE_MODEL * SCALE_MODEL
SHRINK_HIDDEN = INNER_RATE * SCALE_HIDDEN * SCALE_HIDDEN

F32 = jnp.float32
BF16 = jnp.bfloat16


def iota(shape, dim):
    return lax.broadcasted_iota(jnp.int32, shape, dim)


def mm(a, b, adim=1, bdim=0, precision=None):
    return lax.dot_general(
        a, b, (((adim,), (bdim,)), ((), ())), precision=precision, preferred_element_type=F32
    )


def split_two(x):
    high = x.astype(BF16)
    return high, (x - high.astype(F32)).astype(BF16)


def silu_parts(pre):
    sig = jax.nn.sigmoid(pre)
    return pre * sig, sig * (1.0 + pre * (1.0 - sig))


def call(kernel, outs, limit=20, flops=1_000_000_000, bytes_accessed=10_000_000):
    return pl.pallas_call(
        kernel,
        out_shape=outs,
        compiler_params=pltpu.CompilerParams(vmem_limit_bytes=limit * 1024 * 1024),
        cost_estimate=pl.CostEstimate(
            flops=flops, bytes_accessed=bytes_accessed, transcendentals=0
        ),
    )


def sds(shape, dtype):
    return jax.ShapeDtypeStruct(shape, dtype)


def pack_kernel(cap, tokens, targets, ids, weight, table):
    rows = table.shape[0]
    count = 2 * tokens.shape[1]
    half = tokens.shape[1]
    first, second = iota((count, count), 0), iota((count, count), 1)
    ids_row = jnp.concatenate([ids[0], ids[1]], axis=1)
    ids_col = jnp.sum(jnp.where(first == second, ids_row, 0), axis=1, keepdims=True)
    together = (first < half) == (second < half)
    earlier = (ids_col == ids_row) & (first < second) & together
    slot = jnp.sum(jnp.where(earlier, 1, 0), axis=0, keepdims=True)
    step_row = jnp.where(iota((1, count), 1) < half, 0, cap)
    place = ids_row * (4 * cap) + slot + step_row
    row = iota((rows, count), 0)
    put_token = (row == place).astype(BF16)
    put_target = (row == place + 2 * cap).astype(BF16)
    w_row = jnp.concatenate([weight[0:1, :], weight[1:2, :]], axis=1)
    w_col = jnp.sum(jnp.where(first == second, w_row, 0.0), axis=1, keepdims=True)
    high, rest = split_two(w_col)
    rest = w_col - high.astype(F32)
    middle = rest.astype(BF16)
    low = (rest - middle.astype(F32)).astype(BF16)
    lane = iota((count, EXT), 1)
    w_terms = jnp.where(
        lane == 0,
        high.astype(F32),
        jnp.where(lane == 1, middle.astype(F32), jnp.where(lane == 2, low.astype(F32), 0.0)),
    ).astype(BF16)
    step = 512
    for c in range(0, D, step):
        tok = tokens[:, :, c : c + step].reshape(count, step)
        tgt = targets[:, :, c : c + step].reshape(count, step)
        table[:, c : c + step] = (mm(put_token, tok) + mm(put_target, tgt)).astype(BF16)
    table[:, D : D + EXT] = mm(put_target, w_terms).astype(BF16)


def picker(cap, sources, kind):
    rows = sources * cap
    j = iota((rows, 4 * rows), 0)
    source = (j.astype(F32) * (1.0 / cap) + 0.5 / cap).astype(jnp.int32)
    wanted = j + source * (3 * cap) + kind * cap
    return (iota((rows, 4 * rows), 1) == wanted).astype(BF16)


def own_kernel(cap, own, rows_out, w_out):
    half = own.shape[0] // 4
    sources = half // cap
    for k in range(4):
        pick = picker(cap, sources, k)
        rows_out[k * half : (k + 1) * half, :] = mm(pick, own[:, 0:D]).astype(BF16)
        if k >= 2:
            terms = mm(pick, own[:, D : D + EXT])
            w_out[k - 2] = jnp.broadcast_to(jnp.sum(terms, axis=1, keepdims=True), (half, EXT))


def first_kernel(
    cap, own, other, gate, up, down, x_out, partial, sent, act, slope_up, hidden_out
):
    sources = own.shape[0] // (4 * cap)
    pick = picker(cap, sources, 0)
    half = sources * cap
    x_out[0:half, :] = own[0:half, :]
    x_out[half:, :] = mm(pick, other[:, 0:D]).astype(BF16)
    x = x_out[...]
    pre_gate = mm(x, gate[...]) * SCALE_MODEL
    pre_up = mm(x, up[...]) * SCALE_MODEL
    activated, slope = silu_parts(pre_gate)
    act[...] = activated
    slope_up[...] = pre_up * slope
    hidden = (activated * pre_up).astype(BF16)
    hidden_out[...] = hidden
    result = mm(hidden, down[...]) * SCALE_HIDDEN
    partial[...] = result
    sent[...] = result.astype(BF16)


def unpack_kernel(
    cap, own, w_own, other, gate, up, x1, x2_out, t1_out, t2_out, w_out, gate_out, up_out, cross
):
    sources = own.shape[0] // (4 * cap)
    half = sources * cap
    for k, out in ((1, x2_out), (2, t1_out), (3, t2_out)):
        pick = picker(cap, sources, k)
        out[0:half, :] = own[k * half : (k + 1) * half, :]
        out[half:, :] = mm(pick, other[:, 0:D]).astype(BF16)
        if k >= 2:
            terms = mm(pick, other[:, D : D + EXT])
            w_out[k - 2, 0:half, :] = w_own[k - 2]
            w_out[k - 2, half:, :] = jnp.broadcast_to(
                jnp.sum(terms, axis=1, keepdims=True), (half, EXT)
            )
    x2 = x2_out[...]
    gate_out[...] = mm(x2, gate[...]) * SCALE_MODEL
    up_out[...] = mm(x2, up[...]) * SCALE_MODEL
    cross[...] = mm(x2, x1[...], 1, 1)


def cotangent(partial, received, target, weight):
    half = partial.shape[0] // 2
    swapped = jnp.concatenate([received[half:, :], received[:half, :]], axis=0)
    combined = (partial + swapped.astype(F32)).astype(BF16).astype(F32)
    return (weight * (weight * combined - target.astype(F32))).astype(BF16)


def second_kernel(
    partial, received, t1, w, down, act, slope_up, hidden1, gate2, up2, cross,
    cot_out, gate_first_out, up_first_out, partial2, sent, hidden2_out, act2_out, slope_up2_out,
):
    cot = cotangent(partial[...], received[...], t1[...], w[0, :, 0:1])
    cot_out[...] = cot
    hidden_cot = mm(cot, down[...], 1, 1) * SCALE_HIDDEN
    gate_first = (hidden_cot * slope_up[...]).astype(BF16)
    up_first = (hidden_cot * act[...]).astype(BF16)
    gate_first_out[...] = gate_first
    up_first_out[...] = up_first
    high, low = split_two(cross[...])
    pre_gate = gate2[...] - SHRINK_MODEL * (mm(high, gate_first) + mm(low, gate_first))
    pre_up = up2[...] - SHRINK_MODEL * (mm(high, up_first) + mm(low, up_first))
    activated, slope = silu_parts(pre_gate)
    hidden = (activated * pre_up).astype(BF16)
    hidden2_out[...] = hidden
    act2_out[...] = activated
    slope_up2_out[...] = pre_up * slope
    high, low = split_two(mm(hidden, hidden1[...], 1, 1))
    result = mm(hidden, down[...]) * SCALE_HIDDEN - SHRINK_HIDDEN * (mm(high, cot) + mm(low, cot))
    partial2[...] = result
    sent[...] = result.astype(BF16)


def fragment_kernel(
    index, gate, up, down, x1, cot, gate_first, up_first, hidden1, hidden2, act2, slope_up2,
    global_fragment, base, down_part, frag2, hidden_frag2,
):
    start = index[0] * FRAG
    pick = iota((FS, FRAG), 0) == iota((FS, FRAG), 1) + start
    pick_t = (iota((FRAG, FS), 1) == iota((FRAG, FS), 0) + start).astype(BF16)
    pick_f = pick.astype(F32)
    pick = pick.astype(BF16)
    gate_f = mm(gate_first[...], pick).astype(BF16)
    up_f = mm(up_first[...], pick).astype(BF16)
    hidden_f = mm(hidden1[...], pick).astype(BF16)
    base[0] = global_fragment[0] - (
        mm(pick_t, gate[...], 1, 1) - INNER_RATE * (mm(gate_f, x1[...], 0, 0) * SCALE_MODEL)
    )
    base[1] = global_fragment[1] - (
        mm(pick_t, up[...], 1, 1) - INNER_RATE * (mm(up_f, x1[...], 0, 0) * SCALE_MODEL)
    )
    down_rows = mm(pick_t, down[...])
    new_rows = down_rows - INNER_RATE * (mm(hidden_f, cot[...], 0, 0) * SCALE_HIDDEN)
    down_part[...] = new_rows
    base[2] = global_fragment[2] - new_rows
    frag2[0] = mm(slope_up2[...], pick_f, precision=lax.Precision.HIGHEST)
    frag2[1] = mm(act2[...], pick_f, precision=lax.Precision.HIGHEST)
    hidden_frag2[...] = mm(hidden2[...], pick).astype(BF16)


def last_kernel(partial, received, t2, w, x2, down_part, frag2, hidden_frag2, base, out):
    cot = cotangent(partial[...], received[...], t2[...], w[1, :, 0:1])
    high, low = split_two(down_part[...])
    hidden_cot = (mm(cot, high, 1, 1) + mm(cot, low, 1, 1)) * SCALE_HIDDEN
    gate_cot = (hidden_cot * frag2[0]).astype(BF16)
    up_cot = (hidden_cot * frag2[1]).astype(BF16)
    out[0, 0, 0] = base[0] + INNER_RATE * (mm(gate_cot, x2[...], 0, 0) * SCALE_MODEL)
    out[0, 0, 1] = base[1] + INNER_RATE * (mm(up_cot, x2[...], 0, 0) * SCALE_MODEL)
    out[0, 0, 2] = base[2] + INNER_RATE * (mm(hidden_frag2[...], cot, 0, 0) * SCALE_HIDDEN)


def inner_of(replicas):
    return min(replicas, 8)


def mask_of(distance):
    return 12 if distance == 8 else distance


def pick_of(place, distance):
    bit = (place // distance) & 1
    return bit ^ ((place // 8) & 1) if distance == 4 else bit


def swap(values, distance):
    replicas = lax.axis_size("replica")
    return lax.ppermute(values, "replica", [(i, i ^ distance) for i in range(replicas)])


def halve(terms, distance):
    half = terms[0].shape[1] // 2
    bit = pick_of(lax.axis_index("replica"), distance)
    sent = total_of([lax.dynamic_slice_in_dim(t, (1 - bit) * half, half, 1) for t in terms])
    kept = [lax.dynamic_slice_in_dim(t, bit * half, half, 1) for t in terms]
    return kept + [swap(sent.astype(BF16), distance)]


def total_of(terms):
    total = terms[0].astype(F32)
    for term in terms[1:]:
        total = total + term.astype(F32)
    return total


def add_across(values, distance):
    mine = values.astype(BF16)
    return mine.astype(F32) + swap(mine, mask_of(distance)).astype(F32)


def outer_kernel(replicas, marks, me, held_pieces, got_pieces, global_fragment, momentum,
                 new_global, new_momentum):
    rows, lanes = global_fragment.shape
    width = held_pieces.shape[1]
    here = len(marks) // 2 if len(marks) > 1 else 1
    for j, mark in enumerate(marks):
        place = me[0] ^ mark
        lane, step, distance = 0, lanes // 2, 1
        while step >= width:
            lane = lane + pick_of(place, distance) * step
            step //= 2
            distance *= 2
        at = (slice(None), pl.ds(pl.multiple_of(lane, 128), width))
        source, k = (held_pieces, j) if j < here else (got_pieces, j - here)
        mean = source[k * rows : (k + 1) * rows, :].astype(F32) * (1.0 / replicas)
        moved = MOMENTUM * momentum[at] + mean
        new_momentum[at] = moved
        new_global[at] = global_fragment[at] - OUTER_RATE * (mean + MOMENTUM * moved)


def shards(
    tokens,
    targets,
    expert_ids,
    route_weight,
    gate_weight,
    up_weight,
    down_weight,
    fragment_delta,
    global_fragment,
    outer_momentum,
    fragment_index,
):
    size = lax.axis_size("expert")
    experts = size // 2
    replicas = lax.axis_size("replica")
    token_rows = tokens.shape[1]
    cap = 2 * min(token_rows // 2, max(1, token_rows * 3 // (experts * 4)))
    rows = 4 * cap * experts
    slots = 2 * cap * experts
    same_core = [[2 * e + c for e in range(experts)] for c in range(2)]
    pairs = [(i, i ^ 1) for i in range(size)]

    inner = inner_of(replicas)
    terms = halve([fragment_delta.reshape(3 * FRAG, D)], 1)

    table = call(functools.partial(pack_kernel, cap), sds((rows, D + EXT), BF16), 56)(
        tokens, targets, expert_ids.transpose(0, 2, 1), route_weight
    )
    table, terms[-1] = lax.optimization_barrier((table, terms[-1]))
    distance = 2
    while distance < inner:
        terms = halve(terms, distance)
        distance *= 2
    sums = total_of(terms)
    across = []
    while distance < replicas:
        across.insert(0, distance)
        distance *= 2
    for distance in across:
        sums = add_across(sums, distance)
    pieces = sums.astype(BF16)
    own = lax.all_to_all(
        table.reshape(experts, 4 * cap, D + EXT),
        "expert",
        split_axis=0,
        concat_axis=0,
        tiled=True,
        axis_index_groups=same_core,
    ).reshape(rows, D + EXT)
    own, pieces = lax.optimization_barrier((own, pieces))
    other = lax.ppermute(own, "expert", pairs)
    own_rows, w_own = call(
        functools.partial(own_kernel, cap),
        (sds((rows, D), BF16), sds((2, slots // 2, EXT), F32)),
    )(own)
    gather = [inner >> k for k in range(1, inner.bit_length())]
    marks = [0]
    for distance in gather:
        marks += [mark ^ distance for mark in marks]
    held = []
    for distance in gather[:-2]:
        held.append(swap(pieces, distance))
    gate, up, down = gate_weight[0], up_weight[0], down_weight[0]

    x1, partial, sent, act, slope_up, hidden1 = call(
        functools.partial(first_kernel, cap),
        (
            sds((slots, D), BF16),
            sds((slots, D), F32),
            sds((slots, D), BF16),
            sds((slots, FS), F32),
            sds((slots, FS), F32),
            sds((slots, FS), BF16),
        ),
    )(own_rows, other, gate, up, down)
    sent, *held = lax.optimization_barrier((sent, *held))
    for got in held:
        pieces = jnp.concatenate([pieces, got], axis=0)
    received = lax.ppermute(sent, "expert", pairs)
    held = [swap(pieces, distance) for distance in gather[-2:-1]]
    x2, t1, t2, w, gate2, up2, cross = call(
        functools.partial(unpack_kernel, cap),
        (
            sds((slots, D), BF16),
            sds((slots, D), BF16),
            sds((slots, D), BF16),
            sds((2, slots, EXT), F32),
            sds((slots, FS), F32),
            sds((slots, FS), F32),
            sds((slots, slots), F32),
        ),
    )(own_rows, w_own, other, gate, up, x1)
    cot, gate_first, up_first, partial2, sent2, hidden2, act2, slope_up2 = call(
        second_kernel,
        (
            sds((slots, D), BF16),
            sds((slots, FS), BF16),
            sds((slots, FS), BF16),
            sds((slots, D), F32),
            sds((slots, D), BF16),
            sds((slots, FS), BF16),
            sds((slots, FS), F32),
            sds((slots, FS), F32),
        ),
    )(partial, received, t1, w, down, act, slope_up, hidden1, gate2, up2, cross)
    sent2, *held = lax.optimization_barrier((sent2, *held))
    for got in held:
        pieces = jnp.concatenate([pieces, got], axis=0)
    received2 = lax.ppermute(sent2, "expert", pairs)
    got = pieces
    for distance in gather[-1:]:
        got = swap(pieces, distance)
    base, down_part, frag2, hidden_frag2 = pl.pallas_call(
        fragment_kernel,
        out_shape=(
            sds((3, FRAG, D), F32),
            sds((FRAG, D), F32),
            sds((2, slots, FRAG), F32),
            sds((slots, FRAG), BF16),
        ),
        in_specs=[pl.BlockSpec(memory_space=pltpu.SMEM)]
        + [pl.BlockSpec(memory_space=pltpu.VMEM)] * 12,
        compiler_params=pltpu.CompilerParams(vmem_limit_bytes=20 * 1024 * 1024),
        cost_estimate=pl.CostEstimate(
            flops=1_000_000_000, bytes_accessed=10_000_000, transcendentals=0
        ),
    )(
        fragment_index, gate, up, down, x1, cot, gate_first, up_first, hidden1, hidden2, act2,
        slope_up2, global_fragment[0],
    )
    next_delta = call(last_kernel, sds((1, 1, 3, FRAG, D), F32))(
        partial2, received2, t2, w, x2, down_part, frag2, hidden_frag2, base
    )
    next_delta, got = lax.optimization_barrier((next_delta, got))
    new_global, new_momentum = pl.pallas_call(
        functools.partial(outer_kernel, replicas, tuple(marks)),
        out_shape=(sds((3 * FRAG, D), F32), sds((3 * FRAG, D), F32)),
        in_specs=[pl.BlockSpec(memory_space=pltpu.SMEM)]
        + [pl.BlockSpec(memory_space=pltpu.VMEM)] * 4,
        compiler_params=pltpu.CompilerParams(vmem_limit_bytes=20 * 1024 * 1024),
        cost_estimate=pl.CostEstimate(flops=1_000_000_000, bytes_accessed=10_000_000, transcendentals=0),
    )(
        lax.axis_index("replica").astype(jnp.int32).reshape(1),
        pieces,
        got,
        global_fragment.reshape(3 * FRAG, D),
        outer_momentum.reshape(3 * FRAG, D),
    )
    whole = (1, 3, FRAG, D)
    return (next_delta, new_global.reshape(whole), new_momentum.reshape(whole))


def solution(mesh):
    placed = (
        P(None, ("replica", "expert"), None),
        P(None, ("replica", "expert"), None),
        P(None, ("replica", "expert"), None),
        P(None, ("replica", "expert")),
        P("expert", None, None),
        P("expert", None, None),
        P("expert", None, None),
        P("replica", "expert", None, None, None),
        P("expert", None, None, None),
        P("expert", None, None, None),
        P(),
    )
    return jax.shard_map(
        shards,
        mesh=mesh,
        in_specs=placed,
        out_specs=(
            P("replica", "expert", None, None, None),
            P("expert", None, None, None),
            P("expert", None, None, None),
        ),
        check_vma=False,
    )
```

```python
import functools
import math

import jax
import jax.numpy as jnp
from jax import lax
from jax.experimental import pallas as pl
from jax.experimental.pallas import tpu as pltpu
from jax.sharding import PartitionSpec as P

D = 2048
F = 768
FS = 384
FRAG = 32
EXT = 128

INNER_RATE = 0.8
OUTER_RATE = 0.7
MOMENTUM = 0.9
SCALE_MODEL = 1.0 / math.sqrt(D)
SCALE_HIDDEN = 1.0 / math.sqrt(F)
SHRINK_MODEL = INNER_RATE * SCALE_MODEL * SCALE_MODEL
SHRINK_HIDDEN = INNER_RATE * SCALE_HIDDEN * SCALE_HIDDEN

F32 = jnp.float32
BF16 = jnp.bfloat16


def iota(shape, dim):
    return lax.broadcasted_iota(jnp.int32, shape, dim)


def mm(a, b, adim=1, bdim=0, precision=None):
    return lax.dot_general(
        a, b, (((adim,), (bdim,)), ((), ())), precision=precision, preferred_element_type=F32
    )


def split_two(x):
    high = x.astype(BF16)
    return high, (x - high.astype(F32)).astype(BF16)


def silu_parts(pre):
    sig = jax.nn.sigmoid(pre)
    return pre * sig, sig * (1.0 + pre * (1.0 - sig))


def call(kernel, outs, limit=20, flops=1_000_000_000, bytes_accessed=10_000_000):
    return pl.pallas_call(
        kernel,
        out_shape=outs,
        compiler_params=pltpu.CompilerParams(vmem_limit_bytes=limit * 1024 * 1024),
        cost_estimate=pl.CostEstimate(
            flops=flops, bytes_accessed=bytes_accessed, transcendentals=0
        ),
    )


def sds(shape, dtype):
    return jax.ShapeDtypeStruct(shape, dtype)


def pack_kernel(cap, tokens, targets, ids, weight, table):
    rows = table.shape[0]
    count = 2 * tokens.shape[1]
    half = tokens.shape[1]
    first, second = iota((count, count), 0), iota((count, count), 1)
    ids_row = jnp.concatenate([ids[0], ids[1]], axis=1)
    ids_col = jnp.sum(jnp.where(first == second, ids_row, 0), axis=1, keepdims=True)
    together = (first < half) == (second < half)
    earlier = (ids_col == ids_row) & (first < second) & together
    slot = jnp.sum(jnp.where(earlier, 1, 0), axis=0, keepdims=True)
    step_row = jnp.where(iota((1, count), 1) < half, 0, cap)
    place = ids_row * (4 * cap) + slot + step_row
    row = iota((rows, count), 0)
    put_token = (row == place).astype(BF16)
    put_target = (row == place + 2 * cap).astype(BF16)
    w_row = jnp.concatenate([weight[0:1, :], weight[1:2, :]], axis=1)
    w_col = jnp.sum(jnp.where(first == second, w_row, 0.0), axis=1, keepdims=True)
    high, rest = split_two(w_col)
    rest = w_col - high.astype(F32)
    middle = rest.astype(BF16)
    low = (rest - middle.astype(F32)).astype(BF16)
    lane = iota((count, EXT), 1)
    w_terms = jnp.where(
        lane == 0,
        high.astype(F32),
        jnp.where(lane == 1, middle.astype(F32), jnp.where(lane == 2, low.astype(F32), 0.0)),
    ).astype(BF16)
    step = 512
    for c in range(0, D, step):
        tok = tokens[:, :, c : c + step].reshape(count, step)
        tgt = targets[:, :, c : c + step].reshape(count, step)
        table[:, c : c + step] = (mm(put_token, tok) + mm(put_target, tgt)).astype(BF16)
    table[:, D : D + EXT] = mm(put_target, w_terms).astype(BF16)


def picker(cap, sources, kind):
    rows = sources * cap
    j = iota((rows, 4 * rows), 0)
    source = (j.astype(F32) * (1.0 / cap) + 0.5 / cap).astype(jnp.int32)
    wanted = j + source * (3 * cap) + kind * cap
    return (iota((rows, 4 * rows), 1) == wanted).astype(BF16)


def own_kernel(cap, own, rows_out, w_out):
    half = own.shape[0] // 4
    sources = half // cap
    for k in range(4):
        pick = picker(cap, sources, k)
        rows_out[k * half : (k + 1) * half, :] = mm(pick, own[:, 0:D]).astype(BF16)
        if k >= 2:
            terms = mm(pick, own[:, D : D + EXT])
            w_out[k - 2] = jnp.broadcast_to(jnp.sum(terms, axis=1, keepdims=True), (half, EXT))


def first_kernel(
    cap, own, other, gate, up, down, x_out, partial, sent, act, slope_up, hidden_out
):
    sources = own.shape[0] // (4 * cap)
    pick = picker(cap, sources, 0)
    half = sources * cap
    x_out[0:half, :] = own[0:half, :]
    x_out[half:, :] = mm(pick, other[:, 0:D]).astype(BF16)
    x = x_out[...]
    pre_gate = mm(x, gate[...]) * SCALE_MODEL
    pre_up = mm(x, up[...]) * SCALE_MODEL
    activated, slope = silu_parts(pre_gate)
    act[...] = activated
    slope_up[...] = pre_up * slope
    hidden = (activated * pre_up).astype(BF16)
    hidden_out[...] = hidden
    result = mm(hidden, down[...]) * SCALE_HIDDEN
    partial[...] = result
    sent[...] = result.astype(BF16)


def unpack_kernel(
    cap, own, w_own, other, gate, up, x1, x2_out, t1_out, t2_out, w_out, gate_out, up_out, cross
):
    sources = own.shape[0] // (4 * cap)
    half = sources * cap
    for k, out in ((1, x2_out), (2, t1_out), (3, t2_out)):
        pick = picker(cap, sources, k)
        out[0:half, :] = own[k * half : (k + 1) * half, :]
        out[half:, :] = mm(pick, other[:, 0:D]).astype(BF16)
        if k >= 2:
            terms = mm(pick, other[:, D : D + EXT])
            w_out[k - 2, 0:half, :] = w_own[k - 2]
            w_out[k - 2, half:, :] = jnp.broadcast_to(
                jnp.sum(terms, axis=1, keepdims=True), (half, EXT)
            )
    x2 = x2_out[...]
    gate_out[...] = mm(x2, gate[...]) * SCALE_MODEL
    up_out[...] = mm(x2, up[...]) * SCALE_MODEL
    cross[...] = mm(x2, x1[...], 1, 1)


def cotangent(partial, received, target, weight):
    half = partial.shape[0] // 2
    swapped = jnp.concatenate([received[half:, :], received[:half, :]], axis=0)
    combined = (partial + swapped.astype(F32)).astype(BF16).astype(F32)
    return (weight * (weight * combined - target.astype(F32))).astype(BF16)


def second_kernel(
    partial, received, t1, w, down, act, slope_up, hidden1, gate2, up2, cross,
    cot_out, gate_first_out, up_first_out, partial2, sent, hidden2_out, act2_out, slope_up2_out,
):
    cot = cotangent(partial[...], received[...], t1[...], w[0, :, 0:1])
    cot_out[...] = cot
    hidden_cot = mm(cot, down[...], 1, 1) * SCALE_HIDDEN
    gate_first = (hidden_cot * slope_up[...]).astype(BF16)
    up_first = (hidden_cot * act[...]).astype(BF16)
    gate_first_out[...] = gate_first
    up_first_out[...] = up_first
    high, low = split_two(cross[...])
    pre_gate = gate2[...] - SHRINK_MODEL * (mm(high, gate_first) + mm(low, gate_first))
    pre_up = up2[...] - SHRINK_MODEL * (mm(high, up_first) + mm(low, up_first))
    activated, slope = silu_parts(pre_gate)
    hidden = (activated * pre_up).astype(BF16)
    hidden2_out[...] = hidden
    act2_out[...] = activated
    slope_up2_out[...] = pre_up * slope
    high, low = split_two(mm(hidden, hidden1[...], 1, 1))
    result = mm(hidden, down[...]) * SCALE_HIDDEN - SHRINK_HIDDEN * (mm(high, cot) + mm(low, cot))
    partial2[...] = result
    sent[...] = result.astype(BF16)


def start_kernel(index, gate, up, down, global_fragment, base, down_rows):
    start = index[0] * FRAG
    pick = (iota((FRAG, FS), 1) == iota((FRAG, FS), 0) + start).astype(BF16)
    base[0] = global_fragment[0] - mm(pick, gate[...], 1, 1)
    base[1] = global_fragment[1] - mm(pick, up[...], 1, 1)
    rows = mm(pick, down[...])
    base[2] = global_fragment[2] - rows
    down_rows[...] = rows


def fragment_kernel(
    index, x1, cot, gate_first, up_first, hidden1, hidden2, act2, slope_up2, start_base,
    down_rows, base, down_part, frag2, hidden_frag2,
):
    start = index[0] * FRAG
    pick = (iota((FS, FRAG), 0) == iota((FS, FRAG), 1) + start).astype(BF16)
    gate_f = mm(gate_first[...], pick).astype(BF16)
    up_f = mm(up_first[...], pick).astype(BF16)
    hidden_f = mm(hidden1[...], pick).astype(BF16)
    base[0] = start_base[0] + INNER_RATE * (mm(gate_f, x1[...], 0, 0) * SCALE_MODEL)
    base[1] = start_base[1] + INNER_RATE * (mm(up_f, x1[...], 0, 0) * SCALE_MODEL)
    step = INNER_RATE * (mm(hidden_f, cot[...], 0, 0) * SCALE_HIDDEN)
    down_part[...] = down_rows[...] - step
    base[2] = start_base[2] + step
    for k, values in enumerate((slope_up2, act2)):
        high, low = split_two(values[...])
        frag2[k] = mm(high, pick) + mm(low, pick)
    hidden_frag2[...] = mm(hidden2[...], pick).astype(BF16)


def last_kernel(partial, received, t2, w, x2, down_part, frag2, hidden_frag2, base, out):
    cot = cotangent(partial[...], received[...], t2[...], w[1, :, 0:1])
    high, low = split_two(down_part[...])
    hidden_cot = (mm(cot, high, 1, 1) + mm(cot, low, 1, 1)) * SCALE_HIDDEN
    gate_cot = (hidden_cot * frag2[0]).astype(BF16)
    up_cot = (hidden_cot * frag2[1]).astype(BF16)
    out[0, 0, 0] = base[0] + INNER_RATE * (mm(gate_cot, x2[...], 0, 0) * SCALE_MODEL)
    out[0, 0, 1] = base[1] + INNER_RATE * (mm(up_cot, x2[...], 0, 0) * SCALE_MODEL)
    out[0, 0, 2] = base[2] + INNER_RATE * (mm(hidden_frag2[...], cot, 0, 0) * SCALE_HIDDEN)


def inner_of(replicas):
    return min(replicas, 8)


def mask_of(distance):
    return 12 if distance == 8 else distance


def pick_of(place, distance):
    bit = (place // distance) & 1
    return bit ^ ((place // 8) & 1) if distance == 4 else bit


def swap(values, distance):
    replicas = lax.axis_size("replica")
    return lax.ppermute(values, "replica", [(i, i ^ distance) for i in range(replicas)])


def halve(terms, distance):
    half = terms[0].shape[1] // 2
    bit = pick_of(lax.axis_index("replica"), distance)
    sent = total_of([lax.dynamic_slice_in_dim(t, (1 - bit) * half, half, 1) for t in terms])
    kept = [lax.dynamic_slice_in_dim(t, bit * half, half, 1) for t in terms]
    return kept + [swap(sent.astype(BF16), distance)]


def total_of(terms):
    total = terms[0].astype(F32)
    for term in terms[1:]:
        total = total + term.astype(F32)
    return total


def add_across(values, distance):
    mine = values.astype(BF16)
    return mine.astype(F32) + swap(mine, mask_of(distance)).astype(F32)


def outer_kernel(replicas, marks, me, held_pieces, got_pieces, global_fragment, momentum,
                 new_global, new_momentum):
    rows, lanes = global_fragment.shape
    width = held_pieces.shape[1]
    here = len(marks) // 2 if len(marks) > 1 else 1
    for j, mark in enumerate(marks):
        place = me[0] ^ mark
        lane, step, distance = 0, lanes // 2, 1
        while step >= width:
            lane = lane + pick_of(place, distance) * step
            step //= 2
            distance *= 2
        at = (slice(None), pl.ds(pl.multiple_of(lane, 128), width))
        source, k = (held_pieces, j) if j < here else (got_pieces, j - here)
        mean = source[k * rows : (k + 1) * rows, :].astype(F32) * (1.0 / replicas)
        moved = MOMENTUM * momentum[at] + mean
        new_momentum[at] = moved
        new_global[at] = global_fragment[at] - OUTER_RATE * (mean + MOMENTUM * moved)


def shards(
    tokens,
    targets,
    expert_ids,
    route_weight,
    gate_weight,
    up_weight,
    down_weight,
    fragment_delta,
    global_fragment,
    outer_momentum,
    fragment_index,
):
    size = lax.axis_size("expert")
    experts = size // 2
    replicas = lax.axis_size("replica")
    token_rows = tokens.shape[1]
    cap = 2 * min(token_rows // 2, max(1, token_rows * 3 // (experts * 4)))
    rows = 4 * cap * experts
    slots = 2 * cap * experts
    same_core = [[2 * e + c for e in range(experts)] for c in range(2)]
    pairs = [(i, i ^ 1) for i in range(size)]

    inner = inner_of(replicas)
    terms = halve([fragment_delta.reshape(3 * FRAG, D)], 1)

    table = call(functools.partial(pack_kernel, cap), sds((rows, D + EXT), BF16), 56)(
        tokens, targets, expert_ids.transpose(0, 2, 1), route_weight
    )
    table, terms[-1] = lax.optimization_barrier((table, terms[-1]))
    distance = 2
    while distance < inner:
        terms = halve(terms, distance)
        distance *= 2
    sums = total_of(terms)
    across = []
    while distance < replicas:
        across.insert(0, distance)
        distance *= 2
    for distance in across:
        sums = add_across(sums, distance)
    pieces = sums.astype(BF16)
    own = lax.all_to_all(
        table.reshape(experts, 4 * cap, D + EXT),
        "expert",
        split_axis=0,
        concat_axis=0,
        tiled=True,
        axis_index_groups=same_core,
    ).reshape(rows, D + EXT)
    gate, up, down = gate_weight[0], up_weight[0], down_weight[0]
    start_base, down_rows = pl.pallas_call(
        start_kernel,
        out_shape=(sds((3, FRAG, D), F32), sds((FRAG, D), F32)),
        in_specs=[pl.BlockSpec(memory_space=pltpu.SMEM)]
        + [pl.BlockSpec(memory_space=pltpu.VMEM)] * 4,
        compiler_params=pltpu.CompilerParams(vmem_limit_bytes=56 * 1024 * 1024),
        cost_estimate=pl.CostEstimate(
            flops=1_000_000_000, bytes_accessed=10_000_000, transcendentals=0
        ),
    )(fragment_index, gate, up, down, global_fragment[0])
    own, pieces, start_base = lax.optimization_barrier((own, pieces, start_base))
    other = lax.ppermute(own, "expert", pairs)
    own_rows, w_own = call(
        functools.partial(own_kernel, cap),
        (sds((rows, D), BF16), sds((2, slots // 2, EXT), F32)),
    )(own)
    gather = [inner >> k for k in range(1, inner.bit_length())]
    marks = [0]
    for distance in gather:
        marks += [mark ^ distance for mark in marks]
    held = []
    for distance in gather[:-2]:
        held.append(swap(pieces, distance))

    x1, partial, sent, act, slope_up, hidden1 = call(
        functools.partial(first_kernel, cap),
        (
            sds((slots, D), BF16),
            sds((slots, D), F32),
            sds((slots, D), BF16),
            sds((slots, FS), F32),
            sds((slots, FS), F32),
            sds((slots, FS), BF16),
        ),
    )(own_rows, other, gate, up, down)
    sent, *held = lax.optimization_barrier((sent, *held))
    for got in held:
        pieces = jnp.concatenate([pieces, got], axis=0)
    received = lax.ppermute(sent, "expert", pairs)
    held = [swap(pieces, distance) for distance in gather[-2:-1]]
    x2, t1, t2, w, gate2, up2, cross = call(
        functools.partial(unpack_kernel, cap),
        (
            sds((slots, D), BF16),
            sds((slots, D), BF16),
            sds((slots, D), BF16),
            sds((2, slots, EXT), F32),
            sds((slots, FS), F32),
            sds((slots, FS), F32),
            sds((slots, slots), F32),
        ),
    )(own_rows, w_own, other, gate, up, x1)
    cot, gate_first, up_first, partial2, sent2, hidden2, act2, slope_up2 = call(
        second_kernel,
        (
            sds((slots, D), BF16),
            sds((slots, FS), BF16),
            sds((slots, FS), BF16),
            sds((slots, D), F32),
            sds((slots, D), BF16),
            sds((slots, FS), BF16),
            sds((slots, FS), F32),
            sds((slots, FS), F32),
        ),
    )(partial, received, t1, w, down, act, slope_up, hidden1, gate2, up2, cross)
    sent2, *held = lax.optimization_barrier((sent2, *held))
    for got in held:
        pieces = jnp.concatenate([pieces, got], axis=0)
    received2 = lax.ppermute(sent2, "expert", pairs)
    got = pieces
    for distance in gather[-1:]:
        got = swap(pieces, distance)
    base, down_part, frag2, hidden_frag2 = pl.pallas_call(
        fragment_kernel,
        out_shape=(
            sds((3, FRAG, D), F32),
            sds((FRAG, D), F32),
            sds((2, slots, FRAG), F32),
            sds((slots, FRAG), BF16),
        ),
        in_specs=[pl.BlockSpec(memory_space=pltpu.SMEM)]
        + [pl.BlockSpec(memory_space=pltpu.VMEM)] * 10,
        compiler_params=pltpu.CompilerParams(vmem_limit_bytes=20 * 1024 * 1024),
        cost_estimate=pl.CostEstimate(
            flops=1_000_000_000, bytes_accessed=10_000_000, transcendentals=0
        ),
    )(
        fragment_index, x1, cot, gate_first, up_first, hidden1, hidden2, act2, slope_up2,
        start_base, down_rows,
    )
    next_delta = call(last_kernel, sds((1, 1, 3, FRAG, D), F32))(
        partial2, received2, t2, w, x2, down_part, frag2, hidden_frag2, base
    )
    next_delta, got = lax.optimization_barrier((next_delta, got))
    new_global, new_momentum = pl.pallas_call(
        functools.partial(outer_kernel, replicas, tuple(marks)),
        out_shape=(sds((3 * FRAG, D), F32), sds((3 * FRAG, D), F32)),
        in_specs=[pl.BlockSpec(memory_space=pltpu.SMEM)]
        + [pl.BlockSpec(memory_space=pltpu.VMEM)] * 4,
        compiler_params=pltpu.CompilerParams(vmem_limit_bytes=20 * 1024 * 1024),
        cost_estimate=pl.CostEstimate(flops=1_000_000_000, bytes_accessed=10_000_000, transcendentals=0),
    )(
        lax.axis_index("replica").astype(jnp.int32).reshape(1),
        pieces,
        got,
        global_fragment.reshape(3 * FRAG, D),
        outer_momentum.reshape(3 * FRAG, D),
    )
    whole = (1, 3, FRAG, D)
    return (next_delta, new_global.reshape(whole), new_momentum.reshape(whole))


def solution(mesh):
    placed = (
        P(None, ("replica", "expert"), None),
        P(None, ("replica", "expert"), None),
        P(None, ("replica", "expert"), None),
        P(None, ("replica", "expert")),
        P("expert", None, None),
        P("expert", None, None),
        P("expert", None, None),
        P("replica", "expert", None, None, None),
        P("expert", None, None, None),
        P("expert", None, None, None),
        P(),
    )
    return jax.shard_map(
        shards,
        mesh=mesh,
        in_specs=placed,
        out_specs=(
            P("replica", "expert", None, None, None),
            P("expert", None, None, None),
            P("expert", None, None, None),
        ),
        check_vma=False,
    )
```

```python
import functools
import math

import jax
import jax.numpy as jnp
from jax import lax
from jax.experimental import pallas as pl
from jax.experimental.pallas import tpu as pltpu
from jax.sharding import PartitionSpec as P

D = 2048
F = 768
FS = 384
FRAG = 32
EXT = 128

INNER_RATE = 0.8
OUTER_RATE = 0.7
MOMENTUM = 0.9
SCALE_MODEL = 1.0 / math.sqrt(D)
SCALE_HIDDEN = 1.0 / math.sqrt(F)
SHRINK_MODEL = INNER_RATE * SCALE_MODEL * SCALE_MODEL
SHRINK_HIDDEN = INNER_RATE * SCALE_HIDDEN * SCALE_HIDDEN

F32 = jnp.float32
BF16 = jnp.bfloat16


def iota(shape, dim):
    return lax.broadcasted_iota(jnp.int32, shape, dim)


def mm(a, b, adim=1, bdim=0, precision=None):
    return lax.dot_general(
        a, b, (((adim,), (bdim,)), ((), ())), precision=precision, preferred_element_type=F32
    )


def split_two(x):
    high = x.astype(BF16)
    return high, (x - high.astype(F32)).astype(BF16)


def silu_parts(pre):
    sig = jax.nn.sigmoid(pre)
    return pre * sig, sig * (1.0 + pre * (1.0 - sig))


def call(kernel, outs, limit=20, flops=1_000_000_000, bytes_accessed=10_000_000):
    return pl.pallas_call(
        kernel,
        out_shape=outs,
        compiler_params=pltpu.CompilerParams(vmem_limit_bytes=limit * 1024 * 1024),
        cost_estimate=pl.CostEstimate(
            flops=flops, bytes_accessed=bytes_accessed, transcendentals=0
        ),
    )


def sds(shape, dtype):
    return jax.ShapeDtypeStruct(shape, dtype)


def pack_kernel(cap, tokens, targets, ids, weight, table):
    rows = table.shape[0]
    count = 2 * tokens.shape[1]
    half = tokens.shape[1]
    first, second = iota((count, count), 0), iota((count, count), 1)
    ids_row = jnp.concatenate([ids[0], ids[1]], axis=1)
    ids_col = jnp.sum(jnp.where(first == second, ids_row, 0), axis=1, keepdims=True)
    together = (first < half) == (second < half)
    earlier = (ids_col == ids_row) & (first < second) & together
    slot = jnp.sum(jnp.where(earlier, 1, 0), axis=0, keepdims=True)
    step_row = jnp.where(iota((1, count), 1) < half, 0, cap)
    place = ids_row * (4 * cap) + slot + step_row
    row = iota((rows, count), 0)
    put_token = (row == place).astype(BF16)
    put_target = (row == place + 2 * cap).astype(BF16)
    w_row = jnp.concatenate([weight[0:1, :], weight[1:2, :]], axis=1)
    w_col = jnp.sum(jnp.where(first == second, w_row, 0.0), axis=1, keepdims=True)
    high, rest = split_two(w_col)
    rest = w_col - high.astype(F32)
    middle = rest.astype(BF16)
    low = (rest - middle.astype(F32)).astype(BF16)
    lane = iota((count, EXT), 1)
    w_terms = jnp.where(
        lane == 0,
        high.astype(F32),
        jnp.where(lane == 1, middle.astype(F32), jnp.where(lane == 2, low.astype(F32), 0.0)),
    ).astype(BF16)
    step = 512
    for c in range(0, D, step):
        tok = tokens[:, :, c : c + step].reshape(count, step)
        tgt = targets[:, :, c : c + step].reshape(count, step)
        table[:, c : c + step] = (mm(put_token, tok) + mm(put_target, tgt)).astype(BF16)
    table[:, D : D + EXT] = mm(put_target, w_terms).astype(BF16)


def picker(cap, sources, kind):
    rows = sources * cap
    j = iota((rows, 4 * rows), 0)
    source = (j.astype(F32) * (1.0 / cap) + 0.5 / cap).astype(jnp.int32)
    wanted = j + source * (3 * cap) + kind * cap
    return (iota((rows, 4 * rows), 1) == wanted).astype(BF16)


def first_kernel(
    cap, own, other, gate, up, down, x_out, partial, sent, act, slope_up, hidden_out
):
    sources = own.shape[0] // (4 * cap)
    pick = picker(cap, sources, 0)
    half = sources * cap
    x_out[0:half, :] = mm(pick, own[:, 0:D]).astype(BF16)
    x_out[half:, :] = mm(pick, other[:, 0:D]).astype(BF16)
    x = x_out[...]
    pre_gate = mm(x, gate[...]) * SCALE_MODEL
    pre_up = mm(x, up[...]) * SCALE_MODEL
    activated, slope = silu_parts(pre_gate)
    act[...] = activated
    slope_up[...] = pre_up * slope
    hidden = (activated * pre_up).astype(BF16)
    hidden_out[...] = hidden
    result = mm(hidden, down[...]) * SCALE_HIDDEN
    partial[...] = result
    sent[...] = result.astype(BF16)


def unpack_kernel(
    cap, own, other, gate, up, x1, x2_out, t1_out, t2_out, w_out, gate_out, up_out, cross
):
    sources = own.shape[0] // (4 * cap)
    half = sources * cap
    pick = picker(cap, sources, 1)
    x2_out[0:half, :] = mm(pick, own[:, 0:D]).astype(BF16)
    x2_out[half:, :] = mm(pick, other[:, 0:D]).astype(BF16)
    for k, t_out in ((2, t1_out), (3, t2_out)):
        pick = picker(cap, sources, k)
        for part, ref in ((0, own), (half, other)):
            t_out[part : part + half, :] = mm(pick, ref[:, 0:D]).astype(BF16)
            terms = mm(pick, ref[:, D : D + EXT])
            w_out[k - 2, part : part + half, :] = jnp.broadcast_to(
                jnp.sum(terms, axis=1, keepdims=True), (half, EXT)
            )
    x2 = x2_out[...]
    gate_out[...] = mm(x2, gate[...]) * SCALE_MODEL
    up_out[...] = mm(x2, up[...]) * SCALE_MODEL
    cross[...] = mm(x2, x1[...], 1, 1)


def cotangent(partial, received, target, weight):
    half = partial.shape[0] // 2
    swapped = jnp.concatenate([received[half:, :], received[:half, :]], axis=0)
    combined = (partial + swapped.astype(F32)).astype(BF16).astype(F32)
    return (weight * (weight * combined - target.astype(F32))).astype(BF16)


def second_kernel(
    partial, received, t1, w, down, act, slope_up, hidden1, gate2, up2, cross,
    cot_out, gate_first_out, up_first_out, partial2, sent, hidden2_out, act2_out, slope_up2_out,
):
    cot = cotangent(partial[...], received[...], t1[...], w[0, :, 0:1])
    cot_out[...] = cot
    hidden_cot = mm(cot, down[...], 1, 1) * SCALE_HIDDEN
    gate_first = (hidden_cot * slope_up[...]).astype(BF16)
    up_first = (hidden_cot * act[...]).astype(BF16)
    gate_first_out[...] = gate_first
    up_first_out[...] = up_first
    high, low = split_two(cross[...])
    pre_gate = gate2[...] - SHRINK_MODEL * (mm(high, gate_first) + mm(low, gate_first))
    pre_up = up2[...] - SHRINK_MODEL * (mm(high, up_first) + mm(low, up_first))
    activated, slope = silu_parts(pre_gate)
    hidden = (activated * pre_up).astype(BF16)
    hidden2_out[...] = hidden
    act2_out[...] = activated
    slope_up2_out[...] = pre_up * slope
    high, low = split_two(mm(hidden, hidden1[...], 1, 1))
    result = mm(hidden, down[...]) * SCALE_HIDDEN - SHRINK_HIDDEN * (mm(high, cot) + mm(low, cot))
    partial2[...] = result
    sent[...] = result.astype(BF16)


def fragment_kernel(
    index, gate, up, down, x1, cot, gate_first, up_first, hidden1, hidden2, act2, slope_up2,
    global_fragment, base, down_part, frag2, hidden_frag2,
):
    start = index[0] * FRAG
    pick = iota((FS, FRAG), 0) == iota((FS, FRAG), 1) + start
    pick_t = (iota((FRAG, FS), 1) == iota((FRAG, FS), 0) + start).astype(BF16)
    pick = pick.astype(BF16)
    gate_f = mm(gate_first[...], pick).astype(BF16)
    up_f = mm(up_first[...], pick).astype(BF16)
    hidden_f = mm(hidden1[...], pick).astype(BF16)
    base[0] = global_fragment[0] - (
        mm(pick_t, gate[...], 1, 1) - INNER_RATE * (mm(gate_f, x1[...], 0, 0) * SCALE_MODEL)
    )
    base[1] = global_fragment[1] - (
        mm(pick_t, up[...], 1, 1) - INNER_RATE * (mm(up_f, x1[...], 0, 0) * SCALE_MODEL)
    )
    down_rows = mm(pick_t, down[...])
    new_rows = down_rows - INNER_RATE * (mm(hidden_f, cot[...], 0, 0) * SCALE_HIDDEN)
    down_part[...] = new_rows
    base[2] = global_fragment[2] - new_rows
    for k, values in enumerate((slope_up2, act2)):
        high, low = split_two(values[...])
        frag2[k] = mm(high, pick) + mm(low, pick)
    hidden_frag2[...] = mm(hidden2[...], pick).astype(BF16)


def last_kernel(partial, received, t2, w, x2, down_part, frag2, hidden_frag2, base, out):
    cot = cotangent(partial[...], received[...], t2[...], w[1, :, 0:1])
    high, low = split_two(down_part[...])
    hidden_cot = (mm(cot, high, 1, 1) + mm(cot, low, 1, 1)) * SCALE_HIDDEN
    gate_cot = (hidden_cot * frag2[0]).astype(BF16)
    up_cot = (hidden_cot * frag2[1]).astype(BF16)
    out[0, 0, 0] = base[0] + INNER_RATE * (mm(gate_cot, x2[...], 0, 0) * SCALE_MODEL)
    out[0, 0, 1] = base[1] + INNER_RATE * (mm(up_cot, x2[...], 0, 0) * SCALE_MODEL)
    out[0, 0, 2] = base[2] + INNER_RATE * (mm(hidden_frag2[...], cot, 0, 0) * SCALE_HIDDEN)


def inner_of(replicas):
    return min(replicas, 8)


def mask_of(distance):
    return 12 if distance == 8 else distance


def pick_of(place, distance):
    bit = (place // distance) & 1
    return bit ^ ((place // 8) & 1) if distance == 4 else bit


def swap(values, distance):
    replicas = lax.axis_size("replica")
    return lax.ppermute(values, "replica", [(i, i ^ distance) for i in range(replicas)])


def halve(terms, distance):
    half = terms[0].shape[1] // 2
    bit = pick_of(lax.axis_index("replica"), distance)
    sent = total_of([lax.dynamic_slice_in_dim(t, (1 - bit) * half, half, 1) for t in terms])
    kept = [lax.dynamic_slice_in_dim(t, bit * half, half, 1) for t in terms]
    return kept + [swap(sent.astype(BF16), distance)]


def total_of(terms):
    total = terms[0].astype(F32)
    for term in terms[1:]:
        total = total + term.astype(F32)
    return total


def add_across(values, distance):
    mine = values.astype(BF16)
    return mine.astype(F32) + swap(mine, mask_of(distance)).astype(F32)


def outer_kernel(replicas, marks, me, held_pieces, got_pieces, global_fragment, momentum,
                 new_global, new_momentum):
    rows, lanes = global_fragment.shape
    width = held_pieces.shape[1]
    here = len(marks) // 2 if len(marks) > 1 else 1
    for j, mark in enumerate(marks):
        place = me[0] ^ mark
        lane, step, distance = 0, lanes // 2, 1
        while step >= width:
            lane = lane + pick_of(place, distance) * step
            step //= 2
            distance *= 2
        at = (slice(None), pl.ds(pl.multiple_of(lane, 128), width))
        source, k = (held_pieces, j) if j < here else (got_pieces, j - here)
        mean = source[k * rows : (k + 1) * rows, :].astype(F32) * (1.0 / replicas)
        moved = MOMENTUM * momentum[at] + mean
        new_momentum[at] = moved
        new_global[at] = global_fragment[at] - OUTER_RATE * (mean + MOMENTUM * moved)


def shards(
    tokens,
    targets,
    expert_ids,
    route_weight,
    gate_weight,
    up_weight,
    down_weight,
    fragment_delta,
    global_fragment,
    outer_momentum,
    fragment_index,
):
    size = lax.axis_size("expert")
    experts = size // 2
    replicas = lax.axis_size("replica")
    token_rows = tokens.shape[1]
    cap = 2 * min(token_rows // 2, max(1, token_rows * 3 // (experts * 4)))
    rows = 4 * cap * experts
    slots = 2 * cap * experts
    same_core = [[2 * e + c for e in range(experts)] for c in range(2)]
    pairs = [(i, i ^ 1) for i in range(size)]

    inner = inner_of(replicas)
    terms = halve([fragment_delta.reshape(3 * FRAG, D)], 1)

    table = call(functools.partial(pack_kernel, cap), sds((rows, D + EXT), BF16), 56)(
        tokens, targets, expert_ids.transpose(0, 2, 1), route_weight
    )
    table, terms[-1] = lax.optimization_barrier((table, terms[-1]))
    distance = 2
    while distance < inner:
        terms = halve(terms, distance)
        distance *= 2
    sums = total_of(terms)
    across = []
    while distance < replicas:
        across.insert(0, distance)
        distance *= 2
    for distance in across:
        sums = add_across(sums, distance)
    pieces = sums.astype(BF16)
    own = lax.all_to_all(
        table.reshape(experts, 4 * cap, D + EXT),
        "expert",
        split_axis=0,
        concat_axis=0,
        tiled=True,
        axis_index_groups=same_core,
    ).reshape(rows, D + EXT)
    own, pieces = lax.optimization_barrier((own, pieces))
    other = lax.ppermute(own, "expert", pairs)
    gather = [inner >> k for k in range(1, inner.bit_length())]
    marks = [0]
    for distance in gather:
        marks += [mark ^ distance for mark in marks]
    held = []
    for distance in gather[:-2]:
        held.append(swap(pieces, distance))
    gate, up, down = gate_weight[0], up_weight[0], down_weight[0]

    x1, partial, sent, act, slope_up, hidden1 = call(
        functools.partial(first_kernel, cap),
        (
            sds((slots, D), BF16),
            sds((slots, D), F32),
            sds((slots, D), BF16),
            sds((slots, FS), F32),
            sds((slots, FS), F32),
            sds((slots, FS), BF16),
        ),
    )(own, other, gate, up, down)
    sent, *held = lax.optimization_barrier((sent, *held))
    for got in held:
        pieces = jnp.concatenate([pieces, got], axis=0)
    received = lax.ppermute(sent, "expert", pairs)
    held = [swap(pieces, distance) for distance in gather[-2:-1]]
    x2, t1, t2, w, gate2, up2, cross = call(
        functools.partial(unpack_kernel, cap),
        (
            sds((slots, D), BF16),
            sds((slots, D), BF16),
            sds((slots, D), BF16),
            sds((2, slots, EXT), F32),
            sds((slots, FS), F32),
            sds((slots, FS), F32),
            sds((slots, slots), F32),
        ),
    )(own, other, gate, up, x1)
    cot, gate_first, up_first, partial2, sent2, hidden2, act2, slope_up2 = call(
        second_kernel,
        (
            sds((slots, D), BF16),
            sds((slots, FS), BF16),
            sds((slots, FS), BF16),
            sds((slots, D), F32),
            sds((slots, D), BF16),
            sds((slots, FS), BF16),
            sds((slots, FS), F32),
            sds((slots, FS), F32),
        ),
    )(partial, received, t1, w, down, act, slope_up, hidden1, gate2, up2, cross)
    sent2, *held = lax.optimization_barrier((sent2, *held))
    for got in held:
        pieces = jnp.concatenate([pieces, got], axis=0)
    received2 = lax.ppermute(sent2, "expert", pairs)
    got = pieces
    for distance in gather[-1:]:
        got = swap(pieces, distance)
    base, down_part, frag2, hidden_frag2 = pl.pallas_call(
        fragment_kernel,
        out_shape=(
            sds((3, FRAG, D), F32),
            sds((FRAG, D), F32),
            sds((2, slots, FRAG), F32),
            sds((slots, FRAG), BF16),
        ),
        in_specs=[pl.BlockSpec(memory_space=pltpu.SMEM)]
        + [pl.BlockSpec(memory_space=pltpu.VMEM)] * 12,
        compiler_params=pltpu.CompilerParams(vmem_limit_bytes=20 * 1024 * 1024),
        cost_estimate=pl.CostEstimate(
            flops=1_000_000_000, bytes_accessed=10_000_000, transcendentals=0
        ),
    )(
        fragment_index, gate, up, down, x1, cot, gate_first, up_first, hidden1, hidden2, act2,
        slope_up2, global_fragment[0],
    )
    next_delta = call(last_kernel, sds((1, 1, 3, FRAG, D), F32))(
        partial2, received2, t2, w, x2, down_part, frag2, hidden_frag2, base
    )
    next_delta, got = lax.optimization_barrier((next_delta, got))
    new_global, new_momentum = pl.pallas_call(
        functools.partial(outer_kernel, replicas, tuple(marks)),
        out_shape=(sds((3 * FRAG, D), F32), sds((3 * FRAG, D), F32)),
        in_specs=[pl.BlockSpec(memory_space=pltpu.SMEM)]
        + [pl.BlockSpec(memory_space=pltpu.VMEM)] * 4,
        compiler_params=pltpu.CompilerParams(vmem_limit_bytes=20 * 1024 * 1024),
        cost_estimate=pl.CostEstimate(flops=1_000_000_000, bytes_accessed=10_000_000, transcendentals=0),
    )(
        lax.axis_index("replica").astype(jnp.int32).reshape(1),
        pieces,
        got,
        global_fragment.reshape(3 * FRAG, D),
        outer_momentum.reshape(3 * FRAG, D),
    )
    whole = (1, 3, FRAG, D)
    return (next_delta, new_global.reshape(whole), new_momentum.reshape(whole))


def solution(mesh):
    placed = (
        P(None, ("replica", "expert"), None),
        P(None, ("replica", "expert"), None),
        P(None, ("replica", "expert"), None),
        P(None, ("replica", "expert")),
        P("expert", None, None),
        P("expert", None, None),
        P("expert", None, None),
        P("replica", "expert", None, None, None),
        P("expert", None, None, None),
        P("expert", None, None, None),
        P(),
    )
    return jax.shard_map(
        shards,
        mesh=mesh,
        in_specs=placed,
        out_specs=(
            P("replica", "expert", None, None, None),
            P("expert", None, None, None),
            P("expert", None, None, None),
        ),
        check_vma=False,
    )
```
